32 devices in a mesh: rep: 2 (over y), lab: 16 (over z, x, core).
Axes of the slice: x: 2, y: 2, z: 4, core: 2. Of those that a mesh axis runs over, the one named last changes fastest.
Arguments:
- queries: bfloat16 [4096, 768], P(('rep', 'lab')), may hold values from -6 to 6
- shortlist: int32 [4096, 8], P(('rep', 'lab')), may hold values from 0 to 127, all different within a row; in each aligned block of 128 rows (0 to 127, 128 to 255, ...) at most 8 rows name the same one
- positive: int32 [4096, 8], P(('rep', 'lab')), may hold values from 0 to 255
- label_weight: bfloat16 [16384, 768], P('lab'), may hold values from -0.21875 to 0.21875
- first_moment: float32 [2, 8192, 768], P('rep', 'lab'), may hold values from -6 to 6
- second_moment: float32 [2, 8192, 768], P('rep', 'lab'), may hold values from 0.5 to 8
Outputs:
- query_grad: float32 [4096, 768], P(('rep', 'lab'))
- new_weight: float32 [16384, 768], P('lab')
- new_first: float32 [2, 8192, 768], P('rep', 'lab')
- new_second: float32 [2, 8192, 768], P('rep', 'lab')
The draws below stay inside these ranges and needn't reach their ends.
Inputs may be any that keep to these rules, and one draw needn't show every extreme that they name: `shortlist`: the 8 blocks of one query are distinct; among the 128 rows of one device (aligned blocks of rows) no block is named by more than 8 rows, and some block is named by exactly 8.
All inputs are finite; a program needn't handle non-finite values.
Results may differ from the reference program's by a relative error of at most 0.0026.
Values may be sent and summed in bfloat16 or wider, within the bound.
A program may use at most 64 MiB of HBM per device.

```python
import math
import jax
import jax.numpy as jnp
import numpy as np
from jax import lax

D = 768
BLOCK = 128
K = 8
CAP = 8
Q_DEV = 128
NBLK = 128
LABELS = 16384
QUERIES = 4096
SUB = 512
N_REP = 2
N_LAB = 16


def plant(values, own_key, low, top_value):
    dims = values.shape
    place = [jax.random.randint(jax.random.fold_in(own_key, axis), (), 0, dims[axis]) for axis in range(len(dims))]
    values = values.at[tuple(place)].set(low)
    longest = dims.index(max(dims))
    place[longest] = (place[longest] + 1) % dims[longest]
    return values.at[tuple(place)].set(top_value)


def level_of(rng, extent, shards, low, high):
    def one(dim, blocks):
        heights = jax.random.uniform(jax.random.fold_in(jax.random.fold_in(rng, 6), dim), (blocks,), jnp.float32, low / len(shards), high / len(shards))
        return jnp.repeat(jnp.exp(heights), extent[dim] // blocks).reshape((-1,) + (1,) * (len(extent) - dim - 1))

    factor_of = one(*shards[0])
    for cut in shards[1:]:
        factor_of = factor_of * one(*cut)
    return factor_of


def assign_block(rng, own, number, rows, count, top, limit, lean):
    ranking = jax.random.permutation(rng, count)
    packed, ordinary = shares(count, rows * top, limit, lean, True), shares(count, rows * top, limit, lean, False)
    places = jnp.arange(count)

    def named(lengths, offset_by):
        used = int((lengths > 0).sum())
        fixed = max(1, used // 4)
        passed = fixed + (places - fixed + offset_by * (used - fixed)) % max(1, count - fixed)
        return jnp.zeros((count,), jnp.int32).at[ranking[jnp.where(places < fixed, places, passed)]].set(jnp.asarray(lengths, jnp.int32))

    lengths = jnp.where(number % 4 == 0, named(packed, number // 4), named(ordinary, number - number // 4 - 1))
    mixed = jax.random.permutation(jax.random.fold_in(own, 3), count)
    giver, receiver = mixed[0:count // 2 * 2:2], mixed[1:count // 2 * 2:2]
    slack = jnp.minimum(lengths[giver] - 1, limit - lengths[receiver]) // 2
    slack = jnp.where((giver == ranking[0]) | (receiver == ranking[0]) | (lengths[receiver] == 0), 0, jnp.maximum(slack, 0))
    passed = jax.random.randint(jax.random.fold_in(own, 4), (count // 2,), 0, 1 << 20) % (slack + 1)
    lengths = lengths.at[giver].add(-passed).at[receiver].add(passed)
    items = jnp.searchsorted(jnp.cumsum(lengths), jnp.arange(rows * top), side="right").astype(jnp.int32)
    grid = items.reshape(top, rows).T
    grid = grid[jax.random.permutation(jax.random.fold_in(own, 1), rows)]
    offset_by = jax.random.randint(jax.random.fold_in(own, 2), (rows, 1), 0, top)
    return jnp.take_along_axis(grid, (jnp.arange(top)[None, :] + offset_by) % top, axis=1)


def shares(amount, total, bound, skew, full):
    portions = [(1 << 20) // math.isqrt(grade ** skew) + 1 for grade in range(1, amount + 1)]
    largest = bound if full else min(bound, max(-(-total // amount), total * portions[0] // sum(portions)))
    least = 1 if total - largest >= amount - 1 else 0
    given, rest = [largest] + [least] * (amount - 1), total - largest - least * (amount - 1)
    while rest > 0:
        candidates = [i for i in range(1, amount) if given[i] < largest] or [i for i in range(1, amount) if given[i] < bound]
        whole, budget = sum([portions[i] for i in candidates]), rest
        for i in candidates:
            more = min(bound - given[i], max(1, budget * portions[i] // whole), rest)
            given[i] = given[i] + more
            rest = rest - more
    return np.array(given)


def normal_values(stream_key, dims, deviation, limit, pieces=(), kind=jnp.bfloat16):
    factor_of = level_of(stream_key, dims, pieces, -0.22, 0.18) if pieces else 1.0
    values = jax.random.normal(stream_key, dims, jnp.float32) * deviation * factor_of
    return jnp.minimum(jnp.maximum(values, -limit), limit).astype(kind)


def setup_inputs(seed: int = 0) -> dict:
    streams_of = jax.random.split(jax.random.key(seed), 7)
    queries = normal_values(streams_of[0], (QUERIES, D), 1.0, 6.0, ((0, 32),))
    shortlist_keys = jax.random.split(jax.random.fold_in(streams_of[1], 1), QUERIES // Q_DEV)
    shortlist_turns = jax.random.permutation(jax.random.fold_in(streams_of[1], 3), QUERIES // Q_DEV)
    shortlist = jax.vmap(lambda own, number: assign_block(jax.random.fold_in(streams_of[1], 2), own, number, Q_DEV, NBLK, K, CAP, 2))(shortlist_keys, shortlist_turns).reshape((QUERIES, K))
    positive = plant(jax.random.randint(streams_of[2], (QUERIES, K), 0, 2 * BLOCK), jax.random.fold_in(streams_of[2], 1), 0, (2 * BLOCK) - 1).astype(jnp.int32)
    label_weight = normal_values(streams_of[3], (LABELS, D), D ** -0.5, 0.21875, ((0, 16),))
    first_moment = normal_values(streams_of[4], (N_REP, LABELS // N_REP, D), 1.0, 6.0, ((0, 2), (1, 16)), jnp.float32)
    second_moment = jnp.clip(jnp.exp(math.log(8.0) - 2.7725887 * jax.random.uniform(streams_of[5], (N_REP, LABELS // N_REP, D), jnp.float32) ** level_of(streams_of[5], (N_REP, LABELS // N_REP, D), ((0, 2), (1, 16)), -0.2, 0.2)), 0.5, 8.0)
    return dict(queries=queries, shortlist=shortlist, positive=positive, label_weight=label_weight, first_moment=first_moment, second_moment=second_moment)


beta_first = 0.9
beta_second = 0.999
learn_rate = 0.01
adam_epsilon = 1e-08
step_count = 100.0

def reference(queries, shortlist, positive, label_weight, first_moment, second_moment):
    blocks = label_weight.reshape(NBLK, BLOCK, D)
    offsets = jnp.arange(BLOCK, dtype=jnp.int32)
    width = min(64, QUERIES)

    def one_span(carry, inputs):
        rows, block_ids, targets = inputs
        label_tiles = blocks[block_ids].astype(jnp.float32)
        rows_wide = rows.astype(jnp.float32)
        logits = jnp.einsum('cd,ckld->ckl', rows_wide, label_tiles)
        labels = (offsets[None, None, :] == targets[:, :, None]).astype(jnp.float32)
        slopes = (jax.nn.sigmoid(logits) - labels).astype(jnp.bfloat16)
        slopes_wide = slopes.astype(jnp.float32)
        row_parts = jnp.einsum('ckl,ckld->ckd', slopes_wide, label_tiles)
        row_grad = lax.optimization_barrier(jnp.sum(row_parts, axis=1))
        weight_parts = jnp.einsum('ckl,cd->ckld', slopes_wide, rows_wide)
        carry = carry.at[block_ids.reshape(-1)].add(weight_parts.reshape(-1, BLOCK, D))
        return (carry, row_grad)
    start = jnp.zeros((NBLK, BLOCK, D), jnp.float32)
    inputs = (queries.reshape(-1, width, D), shortlist.reshape(-1, width, K), positive.reshape(-1, width, K))
    weight_grad, row_grads = lax.scan(one_span, start, inputs)
    query_grad = row_grads.reshape(QUERIES, D)
    grad_view = weight_grad.reshape(N_LAB, N_REP, SUB, D).transpose(1, 0, 2, 3).reshape(N_REP, LABELS // N_REP, D)
    new_first = beta_first * first_moment + (1.0 - beta_first) * grad_view
    new_second = beta_second * second_moment + (1.0 - beta_second) * grad_view * grad_view
    first_hat = new_first / (1.0 - beta_first ** step_count)
    second_hat = new_second / (1.0 - beta_second ** step_count)
    step_view = first_hat / (jnp.sqrt(second_hat) + adam_epsilon)
    step_rows = step_view.reshape(N_REP, N_LAB, SUB, D).transpose(1, 0, 2, 3).reshape(LABELS, D)
    new_weight = label_weight.astype(jnp.float32) - learn_rate * step_rows
    return (query_grad, new_weight, new_first, new_second)
```

```python
import functools

import jax
import jax.numpy as jnp
from jax import lax
from jax.experimental import pallas as pl
from jax.experimental.pallas import tpu as pltpu
from jax.sharding import PartitionSpec as P

BLOCK = 128
F32 = jnp.float32
BF16 = jnp.bfloat16
MESH = pl.DeviceIdType.MESH

beta_first = 0.9
beta_second = 0.999
learn_rate = 0.01
adam_epsilon = 1e-08
step_count = 100.0


def chip_at(place, chips):
    place = lax.rem(place + 2 * chips, chips)
    back = lax.div(place, chips // 2)
    return 2 * place + back * (2 * (chips - 1 - place) + 1 - 2 * place)


def kernel(
    reps, labs, rows, depth, names, local, shard,
    q_ref, info_ref, w_ref, first_ref, second_ref,
    grad_ref, step_ref, sum_ref,
    qbuf, ibuf, wg, slope, own_part, pair_out, pair_in, ring_out, ring_in,
    wg_out, wg_in, first, second,
    gather_send, gather_recv, note_send, note_recv,
    twin_send, twin_recv, twin_note_send, twin_note_recv,
    part_send, part_recv, ring_send, ring_recv,
    wg_send, wg_recv, step_send, step_recv, load_sem,
):
    chips = labs // 2
    turns = chips // 2
    half = rows // 2
    tile = min(shard, 256)
    piece = min(shard, BLOCK)
    pieces = shard // piece
    rep = lax.axis_index("rep")
    lab = lax.axis_index("lab")
    core = lax.rem(lab, 2)
    chip = lax.div(lab, 2)
    odd = lax.rem(chip, 2)
    rank = lax.div(chip, 2)
    place = rank + odd * (chips - 1 - 2 * rank)
    ahead = (rep, chip_at(place + 1, chips) * 2 + core)
    behind = (rep, chip_at(place - 1, chips) * 2 + core)
    twin = (rep, chip * 2 + 1 - core)
    partners = [(lax.rem(rep + j, reps), lab) for j in range(1, reps)]

    load_first = pltpu.make_async_copy(first_ref, first, load_sem.at[0])
    load_second = pltpu.make_async_copy(second_ref, second, load_sem.at[1])
    load_first.start()
    load_second.start()

    barrier = pltpu.get_barrier_semaphore()
    everyone = [ahead, behind, twin] + partners
    for other in everyone:
        pl.semaphore_signal(barrier, inc=1, device_id=other, device_id_type=MESH)
    qbuf[0:rows, :] = q_ref[...]
    ibuf[0] = info_ref[...]
    pl.semaphore_wait(barrier, len(everyone))

    def remote(src, dst, send, recv, index, device):
        copy = pltpu.make_async_remote_copy(
            src_ref=src, dst_ref=dst, send_sem=send.at[index], recv_sem=recv.at[index],
            device_id=device, device_id_type=MESH,
        )
        copy.start()
        return copy

    def chunk(way, turn):
        if turn == 0:
            return 0
        if turn == turns:
            return 2 + 4 * (turns - 1)
        return 2 + 4 * (turn - 1) + 2 * way

    def sem(way, turn):
        return 2 * turn - 1 + way if turn else 0

    def span(way, turn):
        if turn == turns:
            return (half * way, half)
        return (0, rows)

    gathers, twins, pending = {}, {}, []

    def send_on(way, turn):
        low, count = span(way, turn)
        src, dst = chunk(way, turn - 1), chunk(way, turn)
        k = sem(way, turn)
        device = ahead if way == 0 else behind
        got = [
            remote(
                qbuf.at[pl.ds(src * rows + low, count)], qbuf.at[pl.ds(dst * rows + low, count)],
                gather_send, gather_recv, k, device,
            )
        ]
        if turn < turns or way == 0:
            got.append(remote(ibuf.at[src], ibuf.at[dst], note_send, note_recv, k, device))
        gathers[way, turn] = got

    def send_twin(way, turn):
        low, count = span(way, turn)
        c = chunk(way, turn)
        k = sem(way, turn)
        got = [
            remote(
                qbuf.at[pl.ds(c * rows + low, count)], qbuf.at[pl.ds((c + 1) * rows + low, count)],
                twin_send, twin_recv, k, twin,
            )
        ]
        if turn < turns or way == 0:
            got.append(remote(ibuf.at[c], ibuf.at[c + 1], twin_note_send, twin_note_recv, k, twin))
        twins[way, turn] = got

    def one_tile(group, start):
        low = chunk(0, group)
        count = 2 if group in (0, turns) else 4
        width = count * rows
        queries = qbuf[low * rows : low * rows + width, :]
        listed = jnp.concatenate([ibuf[low + i, 0:names, :] for i in range(count)], axis=1).astype(F32)
        wanted = jnp.concatenate(
            [ibuf[low + i, names : 2 * names, :] for i in range(count)], axis=1
        ).astype(F32)
        logits = lax.dot_general(
            w_ref[pl.ds(start, tile), :], queries, (((1,), (1,)), ((), ())),
            preferred_element_type=F32,
        )
        parts = []
        for c in range(tile // piece):
            label = lab * local + start + c * piece
            block = lax.div(label, BLOCK)
            shift = lax.rem(label, BLOCK).astype(F32)
            mark = jnp.sum(
                jnp.where(listed == block.astype(F32), wanted + 1.0, 0.0), axis=0, keepdims=True
            )
            offsets = lax.broadcasted_iota(jnp.int32, (piece, width), 0).astype(F32) + 1.0
            target = (offsets == mark - shift).astype(F32)
            value = jax.nn.sigmoid(logits[c * piece : (c + 1) * piece, :]) - target
            parts.append(jnp.where(mark > 0.0, value, 0.0).astype(BF16))
        slopes = parts[0] if len(parts) == 1 else jnp.concatenate(parts, axis=0)
        slope[pl.ds(start, tile), 0:width] = slopes
        term = jnp.dot(slopes, queries, preferred_element_type=F32)
        if group == 0:
            wg[pl.ds(start, tile), :] = term
        else:
            wg[pl.ds(start, tile), :] = wg[pl.ds(start, tile), :] + term

    per_shard = shard // tile

    def tile_start(j):
        owner = lax.rem(rep + 1 + lax.div(j, per_shard), reps)
        return pl.multiple_of(owner * shard + lax.rem(j, per_shard) * tile, tile)

    def pair_of(way, turn):
        return chunk(way, turn) // 2

    part_copies = {}

    def row_parts(group):
        ways = (0,) if group in (0, turns) else (0, 1)
        for way in ways:
            i = pair_of(way, group)
            lanes = way * 2 * rows
            part = lax.dot_general(
                slope[:, lanes : lanes + 2 * rows], w_ref[...], (((0,), (0,)), ((), ())),
                preferred_element_type=F32,
            )
            own_part[i] = part[0:rows]
            pair_out[i] = part[rows : 2 * rows].astype(BF16)
            part_copies[i] = remote(
                pair_out.at[i], pair_in.at[i], part_send, part_recv, i, twin
            )

    def wait_twins(group):
        ways = (0,) if group == 0 else (0, 1)
        for way in ways:
            for copy in twins[way, group]:
                copy.wait_recv()

    send_on(0, 1)
    send_on(1, 1)
    send_twin(0, 0)
    for turn in range(1, turns + 1):
        for way in (0, 1):
            for copy in gathers[way, turn]:
                copy.wait_recv()
        for way in (0, 1):
            if turn < turns:
                send_on(way, turn + 1)
            send_twin(way, turn)
        group = turn - 1
        wait_twins(group)

        @pl.loop(0, local // tile)
        def _(j):
            one_tile(group, tile_start(j))

        row_parts(group)
    wait_twins(turns)

    wg_copies = {}
    for j in range(local // tile):
        start = tile_start(j)
        one_tile(turns, start)
        peer = j // per_shard
        if peer < reps - 1:
            low = (j % per_shard) * tile
            wg_out[peer, low : low + tile, :] = wg[pl.ds(start, tile), :].astype(BF16)
            for y in range(low // piece, (low + tile) // piece):
                wg_copies[peer, y] = remote(
                    wg_out.at[peer, pl.ds(y * piece, piece)],
                    wg_in.at[peer, pl.ds(y * piece, piece)],
                    wg_send, wg_recv, peer * pieces + y, partners[peer],
                )
    row_parts(turns)
    load_first.wait()
    load_second.wait()

    ring_copies = {}

    def ring_step(s):
        for way in (0, 1):
            i = pair_of(1 - way, turns - s)
            if s > 0 or way == 0:
                part_copies[i].wait_recv()
            k = way * turns + s
            device = ahead if way == 0 else behind
            if s == 0:
                low = half * way
                value = own_part[i, low : low + half, :] + pair_in[i, low : low + half, :].astype(F32)
                ring_out[k, 0:half, :] = value.astype(BF16)
                ring_copies[way, s] = remote(
                    ring_out.at[k, pl.ds(0, half)], ring_in.at[k, pl.ds(0, half)],
                    ring_send, ring_recv, k, device,
                )
                continue
            ring_copies[way, s - 1].wait_recv()
            value = own_part[i] + pair_in[i].astype(F32)
            if s == 1:
                low = half * way
                came = ring_in[k - 1, 0:half, :].astype(F32)
                mixed = [value[0:half], value[half:rows]]
                mixed[way] = mixed[way] + came
                ring_out[k, 0:half, :] = mixed[0].astype(BF16)
                ring_out[k, half:rows, :] = mixed[1].astype(BF16)
            else:
                ring_out[k] = (value + ring_in[k - 1].astype(F32)).astype(BF16)
            ring_copies[way, s] = remote(
                ring_out.at[k], ring_in.at[k], ring_send, ring_recv, k, device
            )

    def ring_end():
        part_copies[0].wait_recv()
        value = own_part[0] + pair_in[0].astype(F32)
        for way in (0, 1):
            ring_copies[way, turns - 1].wait_recv()
            value = value + ring_in[way * turns + turns - 1].astype(F32)
        grad_ref[...] = value

    step_copies = []

    def adam(y):
        low = y * piece
        here = pl.multiple_of(rep * shard + low, piece)
        total = wg[pl.ds(here, piece), :]
        for peer in range(reps - 1):
            wg_copies[peer, y].wait_recv()
            total = total + wg_in[peer, low : low + piece, :].astype(F32)
        sum_ref[low : low + piece, :] = total
        new_first = beta_first * first[low : low + piece, :] + (1.0 - beta_first) * total
        new_second = beta_second * second[low : low + piece, :] + (1.0 - beta_second) * total * total
        first_hat = new_first * (1.0 / (1.0 - beta_first**step_count))
        second_hat = new_second * (1.0 / (1.0 - beta_second**step_count))
        step_ref[pl.ds(here, piece), :] = (
            first_hat / (jnp.sqrt(second_hat) + adam_epsilon)
        ).astype(BF16)
        for peer in range(reps - 1):
            step_copies.append(
                remote(
                    step_ref.at[pl.ds(here, piece)], step_ref.at[pl.ds(here, piece)],
                    step_send, step_recv, peer * pieces + y, partners[peer],
                )
            )

    ring_step(0)
    ring_step(1)
    for k in range(max(pieces, turns - 1)):
        if k < pieces:
            adam(k)
        if k + 2 < turns:
            ring_step(k + 2)
        if k + 2 == turns:
            ring_end()

    for copies in (gathers, twins):
        for group in copies.values():
            for copy in group:
                copy.wait_send()
    for copies in (part_copies, ring_copies, wg_copies):
        for copy in copies.values():
            copy.wait_send()
    for copy in step_copies:
        copy.wait_send()
        copy.wait_recv()


def body(reps, labs, queries, shortlist, positive, label_weight, first_moment, second_moment):
    rows, depth = queries.shape
    names = shortlist.shape[1]
    local = label_weight.shape[0]
    shard = first_moment.shape[1]
    chips = labs // 2
    turns = chips // 2
    tile = min(shard, 256)
    piece = min(shard, BLOCK)
    pieces = shard // piece
    info = jnp.concatenate([shortlist.T, positive.T], axis=0).astype(BF16)
    vmem = pl.BlockSpec(memory_space=pltpu.VMEM)
    anywhere = pl.BlockSpec(memory_space=pl.ANY)
    dma = pltpu.SemaphoreType.DMA
    scratch = [
        pltpu.VMEM((labs * rows, depth), BF16),
        pltpu.VMEM((labs, 2 * names, rows), BF16),
        pltpu.VMEM((local, depth), F32),
        pltpu.VMEM((local, 4 * rows), BF16),
        pltpu.VMEM((chips, rows, depth), F32),
        pltpu.VMEM((chips, rows, depth), BF16),
        pltpu.VMEM((chips, rows, depth), BF16),
        pltpu.VMEM((2 * turns, rows, depth), BF16),
        pltpu.VMEM((2 * turns, rows, depth), BF16),
        pltpu.VMEM((reps - 1, shard, depth), BF16),
        pltpu.VMEM((reps - 1, shard, depth), BF16),
        pltpu.VMEM((shard, depth), F32),
        pltpu.VMEM((shard, depth), F32),
    ]
    scratch += [dma((2 * turns + 1,))] * 8
    scratch += [dma((chips,))] * 2 + [dma((2 * turns,))] * 2
    scratch += [dma(((reps - 1) * pieces,))] * 4 + [dma((2,))]
    grad, step, total = pl.pallas_call(
        functools.partial(kernel, reps, labs, rows, depth, names, local, shard),
        out_shape=(
            jax.ShapeDtypeStruct((rows, depth), F32),
            jax.ShapeDtypeStruct((local, depth), BF16),
            jax.ShapeDtypeStruct((shard, depth), F32),
        ),
        in_specs=[vmem, vmem, vmem, anywhere, anywhere],
        out_specs=(vmem, vmem, vmem),
        scratch_shapes=scratch,
        compiler_params=pltpu.CompilerParams(
            collective_id=0, has_side_effects=True, vmem_limit_bytes=56 * 1024 * 1024
        ),
    )(queries, info, label_weight, first_moment[0], second_moment[0])
    total = total[None]
    new_first = beta_first * first_moment + (1.0 - beta_first) * total
    new_second = beta_second * second_moment + (1.0 - beta_second) * total * total
    new_weight = label_weight.astype(F32) - learn_rate * step.astype(F32)
    return (grad, new_weight, new_first, new_second)


def solution(mesh):
    in_specs = (
        P(("rep", "lab"), None),
        P(("rep", "lab"), None),
        P(("rep", "lab"), None),
        P("lab", None),
        P("rep", "lab", None),
        P("rep", "lab", None),
    )
    out_specs = (
        P(("rep", "lab"), None),
        P("lab", None),
        P("rep", "lab", None),
        P("rep", "lab", None),
    )
    run = functools.partial(body, mesh.shape["rep"], mesh.shape["lab"])
    return jax.shard_map(run, mesh=mesh, in_specs=in_specs, out_specs=out_specs, check_vma=False)
```

```python
import functools

import jax
import jax.numpy as jnp
from jax import lax
from jax.experimental import pallas as pl
from jax.experimental.pallas import tpu as pltpu
from jax.sharding import PartitionSpec as P

BLOCK = 128
CAP = 8
F32 = jnp.float32
BF16 = jnp.bfloat16
MESH = pl.DeviceIdType.MESH

beta_first = 0.9
beta_second = 0.999
learn_rate = 0.01
adam_epsilon = 1e-08
step_count = 100.0


def chip_at(place, chips):
    place = lax.rem(place + 2 * chips, chips)
    back = lax.div(place, chips // 2)
    return 2 * place + back * (2 * (chips - 1 - place) + 1 - 2 * place)


def kernel(
    reps, labs, rows, depth, names, local, shard,
    q_ref, info_ref, w_ref, first_ref, second_ref,
    grad_ref, step_ref, sum_ref,
    qbuf, ibuf, wg, gbuf, mbuf, pbuf, qslot, earlier, own_part, pair_out, pair_in,
    ring_out, ring_in, last_out, last_in, wg_out, wg_in, first, second,
    gather_send, gather_recv, note_send, note_recv,
    twin_send, twin_recv, twin_note_send, twin_note_recv,
    part_send, part_recv, ring_send, ring_recv,
    wg_send, wg_recv, step_send, step_recv, load_sem,
):
    chips = labs // 2
    turns = chips // 2
    half = rows // 2
    blocks = local // BLOCK
    piece = min(shard, BLOCK)
    pieces = shard // piece
    rep = lax.axis_index("rep")
    lab = lax.axis_index("lab")
    core = lax.rem(lab, 2)
    chip = lax.div(lab, 2)
    odd = lax.rem(chip, 2)
    rank = lax.div(chip, 2)
    place = rank + odd * (chips - 1 - 2 * rank)
    ahead = (rep, chip_at(place + 1, chips) * 2 + core)
    behind = (rep, chip_at(place - 1, chips) * 2 + core)
    twin = (rep, chip * 2 + 1 - core)
    partners = [(lax.rem(rep + j, reps), lab) for j in range(1, reps)]

    load_first = pltpu.make_async_copy(first_ref, first, load_sem.at[0])
    load_second = pltpu.make_async_copy(second_ref, second, load_sem.at[1])
    load_first.start()
    load_second.start()

    barrier = pltpu.get_barrier_semaphore()
    everyone = [ahead, behind, twin] + partners
    for other in everyone:
        pl.semaphore_signal(barrier, inc=1, device_id=other, device_id_type=MESH)
    qbuf[0:rows, :] = q_ref[...]
    ibuf[0] = info_ref[...]
    pl.semaphore_wait(barrier, len(everyone))

    def remote(src, dst, send, recv, index, device):
        copy = pltpu.make_async_remote_copy(
            src_ref=src, dst_ref=dst, send_sem=send.at[index], recv_sem=recv.at[index],
            device_id=device, device_id_type=MESH,
        )
        copy.start()
        return copy

    def chunk(way, turn):
        if turn == 0:
            return 0
        if turn == turns:
            return 2 + 4 * (turns - 1)
        return 2 + 4 * (turn - 1) + 2 * way

    def sem(way, turn):
        return 2 * turn - 1 + way if turn else 0

    gathers, twins = {}, {}
    slots = 2 * CAP

    def halves(way, turn):
        return (way,) if turn == turns else (0, 1)

    def send_on(way, turn, part):
        src, dst = chunk(way, turn - 1), chunk(way, turn)
        k = 2 * sem(way, turn) + part
        device = ahead if way == 0 else behind
        low = part * half
        got = [
            remote(
                qbuf.at[pl.ds(src * rows + low, half)], qbuf.at[pl.ds(dst * rows + low, half)],
                gather_send, gather_recv, k, device,
            )
        ]
        if part == 0:
            got.append(remote(ibuf.at[src], ibuf.at[dst], note_send, note_recv, k, device))
        gathers[way, turn, part] = got

    def send_twin(way, turn, part):
        c = chunk(way, turn)
        k = 2 * sem(way, turn) + part
        low = part * half
        got = [
            remote(
                qbuf.at[pl.ds(c * rows + low, half)], qbuf.at[pl.ds((c + 1) * rows + low, half)],
                twin_send, twin_recv, k, twin,
            )
        ]
        if part == 0:
            got.append(remote(ibuf.at[c], ibuf.at[c + 1], twin_note_send, twin_note_recv, k, twin))
        twins[way, turn, part] = got

    def pair_of(way, turn):
        return chunk(way, turn) // 2

    def pick(i):
        width = 2 * rows
        pair = (2 * i, 2 * i + 1)
        listed = jnp.concatenate([ibuf[c, 0:names, :] for c in pair], axis=1).astype(F32)
        wanted = jnp.concatenate([ibuf[c, names : 2 * names, :] for c in pair], axis=1).astype(F32)
        hits, marks = [], []
        for b in range(blocks):
            same = listed == (lab * blocks + b).astype(F32)
            hits.append(jnp.sum(jnp.where(same, 1.0, 0.0), axis=0, keepdims=True))
            marks.append(jnp.sum(jnp.where(same, wanted + 1.0, 0.0), axis=0, keepdims=True))
        hit = jnp.concatenate(hits, axis=0)
        later = lax.broadcasted_iota(jnp.int32, (blocks, width), 1) >= rows
        order = jnp.dot(hit.astype(BF16), earlier[...], preferred_element_type=F32)
        order = order + jnp.where(later, float(CAP), 0.0)
        order = jnp.where(hit > 0.0, order, -1.0)
        number = lax.broadcasted_iota(jnp.int32, (slots, width), 0).astype(F32)
        chosen = []
        for b in range(blocks):
            mine = number == order[b : b + 1, :]
            mark = jnp.sum(jnp.where(mine, marks[b], 0.0), axis=1, keepdims=True)
            mbuf[b, i * slots : (i + 1) * slots, :] = jnp.broadcast_to(mark, (slots, BLOCK))
            chosen.append(jnp.where(mine, 1.0, 0.0))
        select = jnp.concatenate(chosen, axis=0).astype(BF16)
        pbuf[i] = select
        picked = jnp.dot(
            select, qbuf[2 * i * rows : 2 * (i + 1) * rows, :], preferred_element_type=F32
        ).astype(BF16)
        for b in range(blocks):
            gbuf[b, i * slots : (i + 1) * slots, :] = picked[b * slots : (b + 1) * slots, :]

    def one_block(b):
        rows_in = gbuf[b]
        here = pl.multiple_of(b * BLOCK, BLOCK)
        weights = w_ref[pl.ds(here, BLOCK), :]
        logits = lax.dot_general(
            rows_in, weights, (((1,), (1,)), ((), ())), preferred_element_type=F32
        )
        mark = mbuf[b]
        offsets = lax.broadcasted_iota(jnp.int32, mark.shape, 1).astype(F32) + 1.0
        target = (offsets == mark).astype(F32)
        slopes = jnp.where(mark > 0.0, jax.nn.sigmoid(logits) - target, 0.0).astype(BF16)
        wg[pl.ds(here, BLOCK), :] = lax.dot_general(
            slopes, rows_in, (((0,), (0,)), ((), ())), preferred_element_type=F32
        )
        qslot[b] = jnp.dot(slopes, weights, preferred_element_type=F32)

    part_copies = {}

    def row_parts(i):
        slot_grad = jnp.concatenate(
            [qslot[b, i * slots : (i + 1) * slots, :] for b in range(blocks)], axis=0
        )
        high = slot_grad.astype(BF16)
        low = (slot_grad - high.astype(F32)).astype(BF16)
        dims = (((0,), (0,)), ((), ()))
        part = lax.dot_general(pbuf[i], high, dims, preferred_element_type=F32)
        part = part + lax.dot_general(pbuf[i], low, dims, preferred_element_type=F32)
        own_part[i] = part[0:rows]
        pair_out[i] = part[rows : 2 * rows]
        part_copies[i] = remote(pair_out.at[i], pair_in.at[i], part_send, part_recv, i, twin)

    def pick_turn(turn):
        for way in (0, 1):
            for part in halves(way, turn):
                if (way, turn, part) in twins:
                    for copy in twins[way, turn, part]:
                        copy.wait_recv()
        pick(pair_of(0, turn))
        if 0 < turn < turns:
            pick(pair_of(1, turn))

    for part in (0, 1):
        send_on(0, 1, part)
        send_on(1, 1, part)
    for part in (0, 1):
        send_twin(0, 0, part)
    below = lax.broadcasted_iota(jnp.int32, (2 * rows, 2 * rows), 0)
    right = lax.broadcasted_iota(jnp.int32, (2 * rows, 2 * rows), 1)
    one_shard = lax.div(below, rows) == lax.div(right, rows)
    earlier[...] = jnp.where((below < right) & one_shard, 1.0, 0.0).astype(BF16)
    for turn in range(1, turns + 1):
        for part in (0, 1):
            for way in (0, 1):
                if (way, turn, part) not in gathers:
                    continue
                for copy in gathers[way, turn, part]:
                    copy.wait_recv()
                if turn < turns and part in halves(way, turn + 1):
                    send_on(way, turn + 1, part)
                send_twin(way, turn, part)
        pick_turn(turn - 1)
    pick_turn(turns)

    wg_copies = {}

    def wg_send_on(peer, y):
        low = y * piece
        start = pl.multiple_of(lax.rem(rep + 1 + peer, reps) * shard + low, piece)
        wg_out[peer, low : low + piece, :] = wg[pl.ds(start, piece), :].astype(BF16)
        wg_copies[peer, y] = remote(
            wg_out.at[peer, pl.ds(low, piece)], wg_in.at[peer, pl.ds(low, piece)],
            wg_send, wg_recv, peer * pieces + y, partners[peer],
        )

    if shard >= BLOCK:
        per_shard = shard // BLOCK
        for j in range(blocks):
            peer = j // per_shard
            one_block(lax.rem(rep + 1 + peer, reps) * per_shard + j % per_shard)
            if peer < reps - 1:
                wg_send_on(peer, j % per_shard)
    else:
        for b in range(blocks):
            one_block(b)
        for peer in range(reps - 1):
            wg_send_on(peer, 0)
    for turn in range(turns, -1, -1):
        for way in ((0,) if turn in (0, turns) else (0, 1)):
            row_parts(pair_of(way, turn))
    load_first.wait()
    load_second.wait()

    ring_copies = {}

    def ring_step(s):
        for way in (0, 1):
            i = pair_of(1 - way, turns - s)
            if s > 0 or way == 0:
                part_copies[i].wait_recv()
            k = way * turns + s
            device = ahead if way == 0 else behind
            if s == 0:
                low = half * way
                value = own_part[i, low : low + half, :] + pair_in[i, low : low + half, :]
                ring_out[k, 0:half, :] = value.astype(BF16)
                ring_copies[way, s] = remote(
                    ring_out.at[k, pl.ds(0, half)], ring_in.at[k, pl.ds(0, half)],
                    ring_send, ring_recv, k, device,
                )
                continue
            ring_copies[way, s - 1].wait_recv()
            value = own_part[i] + pair_in[i]
            if s == 1:
                low = half * way
                mixed = [value[0:half], value[half:rows]]
                mixed[way] = mixed[way] + ring_in[k - 1, 0:half, :].astype(F32)
                value = jnp.concatenate(mixed, axis=0)
            else:
                value = value + ring_in[k - 1].astype(F32)
            if s == turns - 1:
                last_out[way] = value
                ring_copies[way, s] = remote(
                    last_out.at[way], last_in.at[way], ring_send, ring_recv, k, device
                )
            else:
                ring_out[k] = value.astype(BF16)
                ring_copies[way, s] = remote(
                    ring_out.at[k], ring_in.at[k], ring_send, ring_recv, k, device
                )

    def ring_end():
        part_copies[0].wait_recv()
        value = own_part[0] + pair_in[0]
        for way in (0, 1):
            ring_copies[way, turns - 1].wait_recv()
            value = value + last_in[way]
        grad_ref[...] = value

    step_copies = []

    def adam(y):
        low = y * piece
        here = pl.multiple_of(rep * shard + low, piece)
        total = wg[pl.ds(here, piece), :]
        for peer in range(reps - 1):
            wg_copies[peer, y].wait_recv()
            total = total + wg_in[peer, low : low + piece, :].astype(F32)
        sum_ref[low : low + piece, :] = total
        new_first = beta_first * first[low : low + piece, :] + (1.0 - beta_first) * total
        new_second = beta_second * second[low : low + piece, :] + (1.0 - beta_second) * total * total
        first_hat = new_first * (1.0 / (1.0 - beta_first**step_count))
        second_hat = new_second * (1.0 / (1.0 - beta_second**step_count))
        step_ref[pl.ds(here, piece), :] = (
            first_hat / (jnp.sqrt(second_hat) + adam_epsilon)
        ).astype(BF16)
        for peer in range(reps - 1):
            step_copies.append(
                remote(
                    step_ref.at[pl.ds(here, piece)], step_ref.at[pl.ds(here, piece)],
                    step_send, step_recv, peer * pieces + y, partners[peer],
                )
            )

    ring_step(0)
    ring_step(1)
    for k in range(max(pieces, turns - 1)):
        if k < pieces:
            adam(k)
        if k + 2 < turns:
            ring_step(k + 2)
        if k + 2 == turns:
            ring_end()

    for copies in (gathers, twins):
        for group in copies.values():
            for copy in group:
                copy.wait_send()
    for copies in (part_copies, ring_copies, wg_copies):
        for copy in copies.values():
            copy.wait_send()
    for copy in step_copies:
        copy.wait_send()
        copy.wait_recv()


def body(reps, labs, queries, shortlist, positive, label_weight, first_moment, second_moment):
    rows, depth = queries.shape
    names = shortlist.shape[1]
    local = label_weight.shape[0]
    shard = first_moment.shape[1]
    chips = labs // 2
    turns = chips // 2
    blocks = local // BLOCK
    piece = min(shard, BLOCK)
    pieces = shard // piece
    info = jnp.concatenate([shortlist.T, positive.T], axis=0).astype(BF16)
    vmem = pl.BlockSpec(memory_space=pltpu.VMEM)
    anywhere = pl.BlockSpec(memory_space=pl.ANY)
    dma = pltpu.SemaphoreType.DMA
    scratch = [
        pltpu.VMEM((labs * rows, depth), BF16),
        pltpu.VMEM((labs, 2 * names, rows), BF16),
        pltpu.VMEM((local, depth), F32),
        pltpu.VMEM((blocks, labs * CAP, depth), BF16),
        pltpu.VMEM((blocks, labs * CAP, BLOCK), F32),
        pltpu.VMEM((chips, blocks * 2 * CAP, 2 * rows), BF16),
        pltpu.VMEM((blocks, labs * CAP, depth), F32),
        pltpu.VMEM((2 * rows, 2 * rows), BF16),
        pltpu.VMEM((chips, rows, depth), F32),
        pltpu.VMEM((chips, rows, depth), F32),
        pltpu.VMEM((chips, rows, depth), F32),
        pltpu.VMEM((2 * turns, rows, depth), BF16),
        pltpu.VMEM((2 * turns, rows, depth), BF16),
        pltpu.VMEM((2, rows, depth), F32),
        pltpu.VMEM((2, rows, depth), F32),
        pltpu.VMEM((reps - 1, shard, depth), BF16),
        pltpu.VMEM((reps - 1, shard, depth), BF16),
        pltpu.VMEM((shard, depth), F32),
        pltpu.VMEM((shard, depth), F32),
    ]
    scratch += [dma((4 * turns + 2,))] * 8
    scratch += [dma((chips,))] * 2 + [dma((2 * turns,))] * 2
    scratch += [dma(((reps - 1) * pieces,))] * 4 + [dma((2,))]
    grad, step, total = pl.pallas_call(
        functools.partial(kernel, reps, labs, rows, depth, names, local, shard),
        out_shape=(
            jax.ShapeDtypeStruct((rows, depth), F32),
            jax.ShapeDtypeStruct((local, depth), BF16),
            jax.ShapeDtypeStruct((shard, depth), F32),
        ),
        in_specs=[vmem, vmem, vmem, anywhere, anywhere],
        out_specs=(vmem, vmem, vmem),
        scratch_shapes=scratch,
        compiler_params=pltpu.CompilerParams(
            collective_id=0, has_side_effects=True, vmem_limit_bytes=56 * 1024 * 1024
        ),
    )(queries, info, label_weight, first_moment[0], second_moment[0])
    total = total[None]
    new_first = beta_first * first_moment + (1.0 - beta_first) * total
    new_second = beta_second * second_moment + (1.0 - beta_second) * total * total
    new_weight = label_weight.astype(F32) - learn_rate * step.astype(F32)
    return (grad, new_weight, new_first, new_second)


def solution(mesh):
    in_specs = (
        P(("rep", "lab"), None),
        P(("rep", "lab"), None),
        P(("rep", "lab"), None),
        P("lab", None),
        P("rep", "lab", None),
        P("rep", "lab", None),
    )
    out_specs = (
        P(("rep", "lab"), None),
        P("lab", None),
        P("rep", "lab", None),
        P("rep", "lab", None),
    )
    run = functools.partial(body, mesh.shape["rep"], mesh.shape["lab"])
    return jax.shard_map(run, mesh=mesh, in_specs=in_specs, out_specs=out_specs, check_vma=False)
```

```python
import functools

import jax
import jax.numpy as jnp
from jax import lax
from jax.experimental import pallas as pl
from jax.experimental.pallas import tpu as pltpu
from jax.sharding import PartitionSpec as P

BLOCK = 128
CAP = 8
F32 = jnp.float32
BF16 = jnp.bfloat16
MESH = pl.DeviceIdType.MESH

beta_first = 0.9
beta_second = 0.999
learn_rate = 0.01
adam_epsilon = 1e-08
step_count = 100.0


def chip_at(place, chips):
    place = lax.rem(place + 2 * chips, chips)
    back = lax.div(place, chips // 2)
    return 2 * place + back * (2 * (chips - 1 - place) + 1 - 2 * place)


def mirrored(reps, shard):
    return reps == 2 and shard % BLOCK == 0


def kernel(
    reps, labs, rows, depth, names, local, shard,
    q_ref, info_ref, w_ref, first_ref, second_ref,
    grad_ref, step_ref, sum_ref,
    qbuf, ibuf, wg, gbuf, mbuf, pbuf, qslot, earlier, own_part, pair_out, pair_in,
    ring_out, ring_in, last_out, last_in, wg_out, wg_in, first, second,
    far_q, far_i, far_g, far_m,
    gather_send, gather_recv, note_send, note_recv,
    twin_send, twin_recv, twin_note_send, twin_note_recv,
    part_send, part_recv, ring_send, ring_recv,
    wg_send, wg_recv, step_send, step_recv, load_sem,
    cross_send, cross_recv, cross_note_send, cross_note_recv,
):
    chips = labs // 2
    turns = chips // 2
    half = rows // 2
    blocks = local // BLOCK
    piece = min(shard, BLOCK)
    pieces = shard // piece
    rep = lax.axis_index("rep")
    lab = lax.axis_index("lab")
    core = lax.rem(lab, 2)
    chip = lax.div(lab, 2)
    odd = lax.rem(chip, 2)
    rank = lax.div(chip, 2)
    place = rank + odd * (chips - 1 - 2 * rank)
    ahead = (rep, chip_at(place + 1, chips) * 2 + core)
    behind = (rep, chip_at(place - 1, chips) * 2 + core)
    twin = (rep, chip * 2 + 1 - core)
    partners = [(lax.rem(rep + j, reps), lab) for j in range(1, reps)]

    load_first = pltpu.make_async_copy(first_ref, first, load_sem.at[0])
    load_second = pltpu.make_async_copy(second_ref, second, load_sem.at[1])
    load_first.start()
    load_second.start()

    barrier = pltpu.get_barrier_semaphore()
    everyone = [ahead, behind, twin] + partners
    for other in everyone:
        pl.semaphore_signal(barrier, inc=1, device_id=other, device_id_type=MESH)
    qbuf[0:rows, :] = q_ref[...]
    ibuf[0] = info_ref[...]
    pl.semaphore_wait(barrier, len(everyone))

    def remote(src, dst, send, recv, index, device):
        copy = pltpu.make_async_remote_copy(
            src_ref=src, dst_ref=dst, send_sem=send.at[index], recv_sem=recv.at[index],
            device_id=device, device_id_type=MESH,
        )
        copy.start()
        return copy

    def chunk(way, turn):
        if turn == 0:
            return 0
        if turn == turns:
            return 2 + 4 * (turns - 1)
        return 2 + 4 * (turn - 1) + 2 * way

    def sem(way, turn):
        return 2 * turn - 1 + way if turn else 0

    mirror = mirrored(reps, shard)
    own_first = rep * (shard // BLOCK)
    crossing = (0, 1, turns - 1)
    both = ((qbuf, ibuf, 0), (far_q, far_i, 4 * turns + 2))
    gathers, twins = {}, {}
    slots = 2 * CAP

    def halves(way, turn):
        return (way,) if turn == turns else (0, 1)

    def send_on(way, turn, part, far=0):
        qb, ib, base = both[far]
        src, dst = chunk(way, turn - 1), chunk(way, turn)
        k = base + 2 * sem(way, turn) + part
        device = ahead if way == 0 else behind
        low = part * half
        got = [
            remote(
                qb.at[pl.ds(src * rows + low, half)], qb.at[pl.ds(dst * rows + low, half)],
                gather_send, gather_recv, k, device,
            )
        ]
        if part == 0:
            got.append(remote(ib.at[src], ib.at[dst], note_send, note_recv, k, device))
        gathers[way, turn, part, far] = got

    def send_across(way, turn, part):
        c = chunk(way, turn)
        k = 2 * sem(way, turn) + part
        here = pl.ds(c * rows + part * half, half)
        got = [remote(qbuf.at[here], far_q.at[here], cross_send, cross_recv, k, partners[0])]
        if part == 0:
            got.append(
                remote(ibuf.at[c], far_i.at[c], cross_note_send, cross_note_recv, k, partners[0])
            )
        gathers[way, turn, part, 1] = got

    def send_twin(way, turn, part, far=0):
        qb, ib, base = both[far]
        c = chunk(way, turn)
        k = base + 2 * sem(way, turn) + part
        low = part * half
        got = [
            remote(
                qb.at[pl.ds(c * rows + low, half)], qb.at[pl.ds((c + 1) * rows + low, half)],
                twin_send, twin_recv, k, twin,
            )
        ]
        if part == 0:
            got.append(remote(ib.at[c], ib.at[c + 1], twin_note_send, twin_note_recv, k, twin))
        twins[way, turn, part, far] = got

    def pair_of(way, turn):
        return chunk(way, turn) // 2

    def pick(i, far=0):
        qb, ib, _ = both[far]
        count = shard // BLOCK if far else blocks
        block0 = lab * blocks + (own_first if far else 0)
        gb, mb = (far_g, far_m) if far else (gbuf, mbuf)
        width = 2 * rows
        pair = (2 * i, 2 * i + 1)
        listed = jnp.concatenate([ib[c, 0:names, :] for c in pair], axis=1).astype(F32)
        wanted = jnp.concatenate([ib[c, names : 2 * names, :] for c in pair], axis=1).astype(F32)
        hits, marks = [], []
        for b in range(count):
            same = listed == (block0 + b).astype(F32)
            hits.append(jnp.sum(jnp.where(same, 1.0, 0.0), axis=0, keepdims=True))
            marks.append(jnp.sum(jnp.where(same, wanted + 1.0, 0.0), axis=0, keepdims=True))
        hit = jnp.concatenate(hits, axis=0)
        later = lax.broadcasted_iota(jnp.int32, (count, width), 1) >= rows
        order = jnp.dot(hit.astype(BF16), earlier[...], preferred_element_type=F32)
        order = order + jnp.where(later, float(CAP), 0.0)
        order = jnp.where(hit > 0.0, order, -1.0)
        number = lax.broadcasted_iota(jnp.int32, (slots, width), 0).astype(F32)
        chosen = []
        for b in range(count):
            mine = number == order[b : b + 1, :]
            mark = jnp.sum(jnp.where(mine, marks[b], 0.0), axis=1, keepdims=True)
            mb[b, i * slots : (i + 1) * slots, :] = jnp.broadcast_to(mark, (slots, BLOCK))
            chosen.append(jnp.where(mine, 1.0, 0.0))
        select = jnp.concatenate(chosen, axis=0).astype(BF16)
        if not far:
            pbuf[i] = select
        picked = jnp.dot(
            select, qb[2 * i * rows : 2 * (i + 1) * rows, :], preferred_element_type=F32
        ).astype(BF16)
        for b in range(count):
            gb[b, i * slots : (i + 1) * slots, :] = picked[b * slots : (b + 1) * slots, :]

    def slopes_of(rows_in, weights, mark):
        logits = lax.dot_general(
            rows_in, weights, (((1,), (1,)), ((), ())), preferred_element_type=F32
        )
        offsets = lax.broadcasted_iota(jnp.int32, mark.shape, 1).astype(F32) + 1.0
        target = (offsets == mark).astype(F32)
        return jnp.where(mark > 0.0, jax.nn.sigmoid(logits) - target, 0.0).astype(BF16)

    def weight_part(slopes, rows_in):
        return lax.dot_general(
            slopes, rows_in, (((0,), (0,)), ((), ())), preferred_element_type=F32
        )

    def one_block(b, with_weights=True):
        rows_in = gbuf[b]
        here = pl.multiple_of(b * BLOCK, BLOCK)
        weights = w_ref[pl.ds(here, BLOCK), :]
        slopes = slopes_of(rows_in, weights, mbuf[b])
        if with_weights:
            wg[pl.ds(here, BLOCK), :] = weight_part(slopes, rows_in)
        qslot[b] = jnp.dot(slopes, weights, preferred_element_type=F32)

    def far_block(j):
        rows_in = far_g[j]
        here = pl.multiple_of((own_first + j) * BLOCK, BLOCK)
        slopes = slopes_of(rows_in, w_ref[pl.ds(here, BLOCK), :], far_m[j])
        wg[pl.ds(here, BLOCK), :] = wg[pl.ds(here, BLOCK), :] + weight_part(slopes, rows_in)

    part_copies = {}

    def row_parts(i):
        slot_grad = jnp.concatenate(
            [qslot[b, i * slots : (i + 1) * slots, :] for b in range(blocks)], axis=0
        )
        high = slot_grad.astype(BF16)
        low = (slot_grad - high.astype(F32)).astype(BF16)
        dims = (((0,), (0,)), ((), ()))
        part = lax.dot_general(pbuf[i], high, dims, preferred_element_type=F32)
        part = part + lax.dot_general(pbuf[i], low, dims, preferred_element_type=F32)
        own_part[i] = part[0:rows]
        pair_out[i] = part[rows : 2 * rows]
        part_copies[i] = remote(pair_out.at[i], pair_in.at[i], part_send, part_recv, i, twin)

    def pick_turn(turn, far=0):
        for way in (0, 1):
            for part in halves(way, turn):
                if (way, turn, part, far) in twins:
                    for copy in twins[way, turn, part, far]:
                        copy.wait_recv()
        pick(pair_of(0, turn), far)
        if 0 < turn < turns:
            pick(pair_of(1, turn), far)

    in_order = ((0, 0), (1, 1), (0, 1), (1, 0))

    def cross_turn(turn):
        for way, part in in_order:
            if turn or not way:
                send_across(way, turn, part)

    def far_arrived(turn, cases=in_order):
        for way, part in cases:
            if (way, turn, part, 1) not in gathers:
                continue
            for copy in gathers[way, turn, part, 1]:
                copy.wait_recv()
            following = turn + 1
            if following <= turns and following not in crossing:
                for on in (0, 1) if turn == 0 else (way,):
                    if part in halves(on, following):
                        send_on(on, following, part, 1)
            send_twin(way, turn, part, 1)

    for part in (0, 1):
        send_on(0, 1, part)
        send_on(1, 1, part)
    if mirror:
        cross_turn(0)
    for part in (0, 1):
        send_twin(0, 0, part)
    below = lax.broadcasted_iota(jnp.int32, (2 * rows, 2 * rows), 0)
    right = lax.broadcasted_iota(jnp.int32, (2 * rows, 2 * rows), 1)
    one_shard = lax.div(below, rows) == lax.div(right, rows)
    earlier[...] = jnp.where((below < right) & one_shard, 1.0, 0.0).astype(BF16)
    for turn in range(1, turns + 1):
        for part in (0, 1):
            for way in (0, 1):
                if (way, turn, part, 0) not in gathers:
                    continue
                for copy in gathers[way, turn, part, 0]:
                    copy.wait_recv()
                if turn < turns and part in halves(way, turn + 1):
                    send_on(way, turn + 1, part)
                send_twin(way, turn, part)
        if mirror and turn in crossing:
            cross_turn(turn)
        pick_turn(turn - 1)
        if mirror and turn == turns - 1:
            for far_turn in (0, 1):
                far_arrived(far_turn)
    if mirror:
        far_arrived(turns - 1, in_order[0:2])
    pick_turn(turns)

    wg_copies = {}

    def wg_send_on(peer, y):
        low = y * piece
        start = pl.multiple_of(lax.rem(rep + 1 + peer, reps) * shard + low, piece)
        wg_out[peer, low : low + piece, :] = wg[pl.ds(start, piece), :].astype(BF16)
        wg_copies[peer, y] = remote(
            wg_out.at[peer, pl.ds(low, piece)], wg_in.at[peer, pl.ds(low, piece)],
            wg_send, wg_recv, peer * pieces + y, partners[peer],
        )

    if mirror:
        per_shard = shard // BLOCK
        for j in range(blocks):
            peer = j // per_shard
            one_block(lax.rem(rep + 1 + peer, reps) * per_shard + j % per_shard, peer > 0)
    elif shard >= BLOCK:
        per_shard = shard // BLOCK
        for j in range(blocks):
            peer = j // per_shard
            one_block(lax.rem(rep + 1 + peer, reps) * per_shard + j % per_shard)
            if peer < reps - 1:
                wg_send_on(peer, j % per_shard)
    else:
        for b in range(blocks):
            one_block(b)
        for peer in range(reps - 1):
            wg_send_on(peer, 0)
    for turn in range(turns, -1, -1):
        for way in ((0,) if turn in (0, turns) else (0, 1)):
            row_parts(pair_of(way, turn))
    load_first.wait()
    load_second.wait()

    ring_copies = {}

    def ring_step(s):
        for way in (0, 1):
            i = pair_of(1 - way, turns - s)
            if s > 0 or way == 0:
                part_copies[i].wait_recv()
            k = way * turns + s
            device = ahead if way == 0 else behind
            if s == 0:
                low = half * way
                value = own_part[i, low : low + half, :] + pair_in[i, low : low + half, :]
                ring_out[k, 0:half, :] = value.astype(BF16)
                ring_copies[way, s] = remote(
                    ring_out.at[k, pl.ds(0, half)], ring_in.at[k, pl.ds(0, half)],
                    ring_send, ring_recv, k, device,
                )
                continue
            ring_copies[way, s - 1].wait_recv()
            value = own_part[i] + pair_in[i]
            if s == 1:
                low = half * way
                mixed = [value[0:half], value[half:rows]]
                mixed[way] = mixed[way] + ring_in[k - 1, 0:half, :].astype(F32)
                value = jnp.concatenate(mixed, axis=0)
            else:
                value = value + ring_in[k - 1].astype(F32)
            if s == turns - 1:
                last_out[way] = value
                ring_copies[way, s] = remote(
                    last_out.at[way], last_in.at[way], ring_send, ring_recv, k, device
                )
            else:
                ring_out[k] = value.astype(BF16)
                ring_copies[way, s] = remote(
                    ring_out.at[k], ring_in.at[k], ring_send, ring_recv, k, device
                )

    def ring_end():
        part_copies[0].wait_recv()
        value = own_part[0] + pair_in[0]
        for way in (0, 1):
            ring_copies[way, turns - 1].wait_recv()
            value = value + last_in[way]
        grad_ref[...] = value

    step_copies = []

    def adam(y):
        low = y * piece
        here = pl.multiple_of(rep * shard + low, piece)
        total = wg[pl.ds(here, piece), :]
        for peer in range(0 if mirror else reps - 1):
            wg_copies[peer, y].wait_recv()
            total = total + wg_in[peer, low : low + piece, :].astype(F32)
        sum_ref[low : low + piece, :] = total
        new_first = beta_first * first[low : low + piece, :] + (1.0 - beta_first) * total
        new_second = beta_second * second[low : low + piece, :] + (1.0 - beta_second) * total * total
        first_hat = new_first * (1.0 / (1.0 - beta_first**step_count))
        second_hat = new_second * (1.0 / (1.0 - beta_second**step_count))
        step_ref[pl.ds(here, piece), :] = (
            first_hat / (jnp.sqrt(second_hat) + adam_epsilon)
        ).astype(BF16)
        for peer in range(reps - 1):
            step_copies.append(
                remote(
                    step_ref.at[pl.ds(here, piece)], step_ref.at[pl.ds(here, piece)],
                    step_send, step_recv, peer * pieces + y, partners[peer],
                )
            )

    ring_step(0)
    if mirror:
        pick_turn(0, 1)
        pick_turn(1, 1)
        far_arrived(turns - 1, in_order[2:4])
        for turn in range(2, turns - 1):
            far_arrived(turn)
        far_arrived(turns)
        for turn in range(2, turns + 1):
            pick_turn(turn, 1)
        far_block(0)
        adam(0)
    ring_step(1)
    for k in range(max(pieces, turns - 1)):
        if mirror and k + 1 < pieces:
            far_block(k + 1)
            adam(k + 1)
        if not mirror and k < pieces:
            adam(k)
        if k + 2 < turns:
            ring_step(k + 2)
        if k + 2 == turns:
            ring_end()

    for copies in (gathers, twins):
        for group in copies.values():
            for copy in group:
                copy.wait_send()
    for copies in (part_copies, ring_copies, wg_copies):
        for copy in copies.values():
            copy.wait_send()
    for copy in step_copies:
        copy.wait_send()
        copy.wait_recv()


def body(reps, labs, queries, shortlist, positive, label_weight, first_moment, second_moment):
    rows, depth = queries.shape
    names = shortlist.shape[1]
    local = label_weight.shape[0]
    shard = first_moment.shape[1]
    chips = labs // 2
    turns = chips // 2
    blocks = local // BLOCK
    piece = min(shard, BLOCK)
    pieces = shard // piece
    info = jnp.concatenate([shortlist.T, positive.T], axis=0).astype(BF16)
    vmem = pl.BlockSpec(memory_space=pltpu.VMEM)
    anywhere = pl.BlockSpec(memory_space=pl.ANY)
    dma = pltpu.SemaphoreType.DMA
    scratch = [
        pltpu.VMEM((labs * rows, depth), BF16),
        pltpu.VMEM((labs, 2 * names, rows), BF16),
        pltpu.VMEM((local, depth), F32),
        pltpu.VMEM((blocks, labs * CAP, depth), BF16),
        pltpu.VMEM((blocks, labs * CAP, BLOCK), F32),
        pltpu.VMEM((chips, blocks * 2 * CAP, 2 * rows), BF16),
        pltpu.VMEM((blocks, labs * CAP, depth), F32),
        pltpu.VMEM((2 * rows, 2 * rows), BF16),
        pltpu.VMEM((chips, rows, depth), F32),
        pltpu.VMEM((chips, rows, depth), F32),
        pltpu.VMEM((chips, rows, depth), F32),
        pltpu.VMEM((2 * turns, rows, depth), BF16),
        pltpu.VMEM((2 * turns, rows, depth), BF16),
        pltpu.VMEM((2, rows, depth), F32),
        pltpu.VMEM((2, rows, depth), F32),
        pltpu.VMEM((reps - 1, shard, depth), BF16),
        pltpu.VMEM((reps - 1, shard, depth), BF16),
        pltpu.VMEM((shard, depth), F32),
        pltpu.VMEM((shard, depth), F32),
    ]
    far_labs, far_blocks = (labs, shard // BLOCK) if mirrored(reps, shard) else (1, 1)
    scratch += [
        pltpu.VMEM((far_labs * rows, depth), BF16),
        pltpu.VMEM((far_labs, 2 * names, rows), BF16),
        pltpu.VMEM((far_blocks, far_labs * CAP, depth), BF16),
        pltpu.VMEM((far_blocks, far_labs * CAP, BLOCK), F32),
    ]
    scratch += [dma((8 * turns + 4,))] * 8
    scratch += [dma((chips,))] * 2 + [dma((2 * turns,))] * 2
    scratch += [dma(((reps - 1) * pieces,))] * 4 + [dma((2,))]
    scratch += [dma((4 * turns + 2,))] * 4
    grad, step, total = pl.pallas_call(
        functools.partial(kernel, reps, labs, rows, depth, names, local, shard),
        out_shape=(
            jax.ShapeDtypeStruct((rows, depth), F32),
            jax.ShapeDtypeStruct((local, depth), BF16),
            jax.ShapeDtypeStruct((shard, depth), F32),
        ),
        in_specs=[vmem, vmem, vmem, anywhere, anywhere],
        out_specs=(vmem, vmem, vmem),
        scratch_shapes=scratch,
        compiler_params=pltpu.CompilerParams(
            collective_id=0, has_side_effects=True, vmem_limit_bytes=56 * 1024 * 1024
        ),
    )(queries, info, label_weight, first_moment[0], second_moment[0])
    total = total[None]
    new_first = beta_first * first_moment + (1.0 - beta_first) * total
    new_second = beta_second * second_moment + (1.0 - beta_second) * total * total
    new_weight = label_weight.astype(F32) - learn_rate * step.astype(F32)
    return (grad, new_weight, new_first, new_second)


def solution(mesh):
    in_specs = (
        P(("rep", "lab"), None),
        P(("rep", "lab"), None),
        P(("rep", "lab"), None),
        P("lab", None),
        P("rep", "lab", None),
        P("rep", "lab", None),
    )
    out_specs = (
        P(("rep", "lab"), None),
        P("lab", None),
        P("rep", "lab", None),
        P("rep", "lab", None),
    )
    run = functools.partial(body, mesh.shape["rep"], mesh.shape["lab"])
    return jax.shard_map(run, mesh=mesh, in_specs=in_specs, out_specs=out_specs, check_vma=False)
```

```python
import functools

import jax
import jax.numpy as jnp
from jax import lax
from jax.experimental import pallas as pl
from jax.experimental.pallas import tpu as pltpu
from jax.sharding import PartitionSpec as P

BLOCK = 128
CAP = 8
F32 = jnp.float32
BF16 = jnp.bfloat16
MESH = pl.DeviceIdType.MESH

beta_first = 0.9
beta_second = 0.999
learn_rate = 0.01
adam_epsilon = 1e-08
step_count = 100.0


def chip_at(place, chips):
    place = lax.rem(place + 2 * chips, chips)
    back = lax.div(place, chips // 2)
    return 2 * place + back * (2 * (chips - 1 - place) + 1 - 2 * place)


def mirrored(reps, shard):
    return reps == 2 and shard % BLOCK == 0


def kernel(
    reps, labs, rows, depth, names, local, shard,
    q_ref, info_ref, w_ref, first_ref, second_ref,
    grad_ref, step_ref, sum_ref,
    qbuf, ibuf, wg, gbuf, mbuf, pbuf, qslot, earlier, own_part, pair_out, pair_in,
    ring_out, ring_in, last_out, last_in, wg_out, wg_in, first, second,
    far_q, far_i, far_g, far_m,
    gather_send, gather_recv, note_send, note_recv,
    twin_send, twin_recv, twin_note_send, twin_note_recv,
    part_send, part_recv, ring_send, ring_recv,
    wg_send, wg_recv, step_send, step_recv, load_sem,
    cross_send, cross_recv, cross_note_send, cross_note_recv,
):
    chips = labs // 2
    turns = chips // 2
    half = rows // 2
    blocks = local // BLOCK
    piece = min(shard, BLOCK)
    pieces = shard // piece
    rep = lax.axis_index("rep")
    lab = lax.axis_index("lab")
    core = lax.rem(lab, 2)
    chip = lax.div(lab, 2)
    odd = lax.rem(chip, 2)
    rank = lax.div(chip, 2)
    place = rank + odd * (chips - 1 - 2 * rank)
    ahead = (rep, chip_at(place + 1, chips) * 2 + core)
    behind = (rep, chip_at(place - 1, chips) * 2 + core)
    twin = (rep, chip * 2 + 1 - core)
    partners = [(lax.rem(rep + j, reps), lab) for j in range(1, reps)]

    load_first = pltpu.make_async_copy(first_ref, first, load_sem.at[0])
    load_second = pltpu.make_async_copy(second_ref, second, load_sem.at[1])
    load_first.start()
    load_second.start()

    barrier = pltpu.get_barrier_semaphore()
    everyone = [ahead, behind, twin] + partners
    for other in everyone:
        pl.semaphore_signal(barrier, inc=1, device_id=other, device_id_type=MESH)
    qbuf[0:rows, :] = q_ref[...]
    ibuf[0] = info_ref[...]
    pl.semaphore_wait(barrier, len(everyone))

    def remote(src, dst, send, recv, index, device):
        copy = pltpu.make_async_remote_copy(
            src_ref=src, dst_ref=dst, send_sem=send.at[index], recv_sem=recv.at[index],
            device_id=device, device_id_type=MESH,
        )
        copy.start()
        return copy

    def chunk(way, turn):
        if turn == 0:
            return 0
        if turn == turns:
            return 2 + 4 * (turns - 1)
        return 2 + 4 * (turn - 1) + 2 * way

    def sem(way, turn):
        return 2 * turn - 1 + way if turn else 0

    mirror = mirrored(reps, shard)
    own_first = rep * (shard // BLOCK)
    both = ((qbuf, ibuf, 0), (far_q, far_i, 4 * turns + 2))
    gathers, twins = {}, {}
    slots = 2 * CAP

    def halves(way, turn):
        return (way,) if turn == turns else (0, 1)

    def send_on(way, turn, part, far=0):
        qb, ib, base = both[far]
        src, dst = chunk(way, turn - 1), chunk(way, turn)
        k = base + 2 * sem(way, turn) + part
        device = ahead if way == 0 else behind
        low = part * half
        got = [
            remote(
                qb.at[pl.ds(src * rows + low, half)], qb.at[pl.ds(dst * rows + low, half)],
                gather_send, gather_recv, k, device,
            )
        ]
        if part == 0:
            got.append(remote(ib.at[src], ib.at[dst], note_send, note_recv, k, device))
        gathers[way, turn, part, far] = got

    def send_across(way, turn, part):
        c = chunk(way, turn)
        k = 2 * sem(way, turn) + part
        here = pl.ds(c * rows + part * half, half)
        got = [remote(qbuf.at[here], far_q.at[here], cross_send, cross_recv, k, partners[0])]
        if part == 0:
            got.append(
                remote(ibuf.at[c], far_i.at[c], cross_note_send, cross_note_recv, k, partners[0])
            )
        gathers[way, turn, part, 1] = got

    def send_twin(way, turn, part, far=0):
        qb, ib, base = both[far]
        c = chunk(way, turn)
        k = base + 2 * sem(way, turn) + part
        low = part * half
        got = [
            remote(
                qb.at[pl.ds(c * rows + low, half)], qb.at[pl.ds((c + 1) * rows + low, half)],
                twin_send, twin_recv, k, twin,
            )
        ]
        if part == 0:
            got.append(remote(ib.at[c], ib.at[c + 1], twin_note_send, twin_note_recv, k, twin))
        twins[way, turn, part, far] = got

    def pair_of(way, turn):
        return chunk(way, turn) // 2

    def pick(i, far=0):
        qb, ib, _ = both[far]
        count = shard // BLOCK if far else blocks
        block0 = lab * blocks + (own_first if far else 0)
        gb, mb = (far_g, far_m) if far else (gbuf, mbuf)
        width = 2 * rows
        pair = (2 * i, 2 * i + 1)
        listed = jnp.concatenate([ib[c, 0:names, :] for c in pair], axis=1).astype(F32)
        wanted = jnp.concatenate([ib[c, names : 2 * names, :] for c in pair], axis=1).astype(F32)
        hits, marks = [], []
        for b in range(count):
            same = listed == (block0 + b).astype(F32)
            hits.append(jnp.sum(jnp.where(same, 1.0, 0.0), axis=0, keepdims=True))
            marks.append(jnp.sum(jnp.where(same, wanted + 1.0, 0.0), axis=0, keepdims=True))
        hit = jnp.concatenate(hits, axis=0)
        later = lax.broadcasted_iota(jnp.int32, (count, width), 1) >= rows
        order = jnp.dot(hit.astype(BF16), earlier[...], preferred_element_type=F32)
        order = order + jnp.where(later, float(CAP), 0.0)
        order = jnp.where(hit > 0.0, order, -1.0)
        number = lax.broadcasted_iota(jnp.int32, (slots, width), 0).astype(F32)
        chosen = []
        for b in range(count):
            mine = number == order[b : b + 1, :]
            mark = jnp.sum(jnp.where(mine, marks[b], 0.0), axis=1, keepdims=True)
            mb[b, i * slots : (i + 1) * slots, :] = jnp.broadcast_to(mark, (slots, BLOCK))
            chosen.append(jnp.where(mine, 1.0, 0.0))
        select = jnp.concatenate(chosen, axis=0).astype(BF16)
        if not far:
            pbuf[i] = select
        picked = jnp.dot(
            select, qb[2 * i * rows : 2 * (i + 1) * rows, :], preferred_element_type=F32
        ).astype(BF16)
        for b in range(count):
            gb[b, i * slots : (i + 1) * slots, :] = picked[b * slots : (b + 1) * slots, :]

    def slopes_of(rows_in, weights, mark):
        logits = lax.dot_general(
            rows_in, weights, (((1,), (1,)), ((), ())), preferred_element_type=F32
        )
        offsets = lax.broadcasted_iota(jnp.int32, mark.shape, 1).astype(F32) + 1.0
        target = (offsets == mark).astype(F32)
        return jnp.where(mark > 0.0, jax.nn.sigmoid(logits) - target, 0.0).astype(BF16)

    def weight_part(slopes, rows_in):
        return lax.dot_general(
            slopes, rows_in, (((0,), (0,)), ((), ())), preferred_element_type=F32
        )

    early = (chips - 1) * slots

    def one_block(b, late, with_weights=True):
        low, high = (early, chips * slots) if late else (0, early)
        rows_in = gbuf[b, low:high, :]
        here = pl.multiple_of(b * BLOCK, BLOCK)
        weights = w_ref[pl.ds(here, BLOCK), :]
        slopes = slopes_of(rows_in, weights, mbuf[b, low:high, :])
        if with_weights:
            part = weight_part(slopes, rows_in)
            if late:
                part = wg[pl.ds(here, BLOCK), :] + part
            wg[pl.ds(here, BLOCK), :] = part
        qslot[b, low:high, :] = jnp.dot(slopes, weights, preferred_element_type=F32)

    def far_block(j):
        rows_in = far_g[j]
        here = pl.multiple_of((own_first + j) * BLOCK, BLOCK)
        slopes = slopes_of(rows_in, w_ref[pl.ds(here, BLOCK), :], far_m[j])
        wg[pl.ds(here, BLOCK), :] = wg[pl.ds(here, BLOCK), :] + weight_part(slopes, rows_in)

    part_copies = {}

    def row_parts(i):
        slot_grad = jnp.concatenate(
            [qslot[b, i * slots : (i + 1) * slots, :] for b in range(blocks)], axis=0
        )
        high = slot_grad.astype(BF16)
        low = (slot_grad - high.astype(F32)).astype(BF16)
        dims = (((0,), (0,)), ((), ()))
        part = lax.dot_general(pbuf[i], high, dims, preferred_element_type=F32)
        part = part + lax.dot_general(pbuf[i], low, dims, preferred_element_type=F32)
        own_part[i] = part[0:rows]
        pair_out[i] = part[rows : 2 * rows]
        part_copies[i] = remote(pair_out.at[i], pair_in.at[i], part_send, part_recv, i, twin)

    def pick_turn(turn, far=0):
        for way in (0, 1):
            for part in halves(way, turn):
                if (way, turn, part, far) in twins:
                    for copy in twins[way, turn, part, far]:
                        copy.wait_recv()
        pick(pair_of(0, turn), far)
        if 0 < turn < turns:
            pick(pair_of(1, turn), far)

    in_order = ((0, 0), (1, 1), (0, 1), (1, 0))

    def crosses(turn, part):
        return turn in (0, 1, turns - 1) or (turn < turns and part == 1)

    def cross_turn(turn):
        for way, part in in_order:
            if (turn or not way) and crosses(turn, part):
                send_across(way, turn, part)

    def far_arrived(turn, cases=in_order):
        for way, part in cases:
            if (way, turn, part, 1) not in gathers:
                continue
            for copy in gathers[way, turn, part, 1]:
                copy.wait_recv()
            following = turn + 1
            if following <= turns and not crosses(following, part):
                for on in (0, 1) if turn == 0 else (way,):
                    if part in halves(on, following):
                        send_on(on, following, part, 1)
            send_twin(way, turn, part, 1)

    for part in (0, 1):
        send_on(0, 1, part)
        send_on(1, 1, part)
    if mirror:
        cross_turn(0)
    for part in (0, 1):
        send_twin(0, 0, part)
    below = lax.broadcasted_iota(jnp.int32, (2 * rows, 2 * rows), 0)
    right = lax.broadcasted_iota(jnp.int32, (2 * rows, 2 * rows), 1)
    one_shard = lax.div(below, rows) == lax.div(right, rows)
    earlier[...] = jnp.where((below < right) & one_shard, 1.0, 0.0).astype(BF16)
    per_shard = max(shard // BLOCK, 1)

    def block_at(j):
        if shard < BLOCK:
            return j
        return lax.rem(rep + 1 + j // per_shard, reps) * per_shard + j % per_shard

    def needed(j):
        return not mirror or j // per_shard > 0

    for turn in range(1, turns + 1):
        for part in (0, 1):
            for way in (0, 1):
                if (way, turn, part, 0) not in gathers:
                    continue
                for copy in gathers[way, turn, part, 0]:
                    copy.wait_recv()
                if turn < turns and part in halves(way, turn + 1):
                    send_on(way, turn + 1, part)
                send_twin(way, turn, part)
        if mirror and turn < turns:
            cross_turn(turn)
        if turn < turns:
            pick_turn(turn - 1)
        if turn == turns - 1:
            if mirror:
                for far_turn in (0, 1):
                    far_arrived(far_turn)
            pick_turn(turn)
            for j in range(blocks):
                one_block(block_at(j), False, needed(j))
            for back in range(turns - 1, -1, -1):
                for way in (0, 1) if back else (0,):
                    row_parts(pair_of(way, back))
    pick_turn(turns)

    wg_copies = {}

    def wg_send_on(peer, y):
        low = y * piece
        start = pl.multiple_of(lax.rem(rep + 1 + peer, reps) * shard + low, piece)
        wg_out[peer, low : low + piece, :] = wg[pl.ds(start, piece), :].astype(BF16)
        wg_copies[peer, y] = remote(
            wg_out.at[peer, pl.ds(low, piece)], wg_in.at[peer, pl.ds(low, piece)],
            wg_send, wg_recv, peer * pieces + y, partners[peer],
        )

    for j in range(blocks):
        one_block(block_at(j), True, needed(j))
        if not mirror and shard >= BLOCK and j // per_shard < reps - 1:
            wg_send_on(j // per_shard, j % per_shard)
    if shard < BLOCK:
        for peer in range(reps - 1):
            wg_send_on(peer, 0)
    row_parts(pair_of(0, turns))
    load_first.wait()
    load_second.wait()

    ring_copies = {}

    ring_order = ((0, 1), (1, 0), (0, 0), (1, 1))

    def ring_step(s):
        for way in (0, 1):
            if s > 0 or way == 0:
                part_copies[pair_of(1 - way, turns - s)].wait_recv()
        for way, part in ring_order:
            if s == 0 and part != way:
                continue
            i = pair_of(1 - way, turns - s)
            k = way * turns + s
            here = pl.ds(part * half, half)
            value = own_part[i, here, :] + pair_in[i, here, :]
            if (way, s - 1, part) in ring_copies:
                ring_copies[way, s - 1, part].wait_recv()
                value = value + ring_in[k - 1, here, :].astype(F32)
            if s == turns - 1:
                last_out[way, here, :] = value
                src, dst = last_out.at[way, here], last_in.at[way, here]
            else:
                ring_out[k, here, :] = value.astype(BF16)
                src, dst = ring_out.at[k, here], ring_in.at[k, here]
            ring_copies[way, s, part] = remote(
                src, dst, ring_send, ring_recv, 2 * k + part, ahead if way == 0 else behind
            )

    def ring_end():
        part_copies[0].wait_recv()
        value = own_part[0] + pair_in[0]
        for way in (0, 1):
            for part in (0, 1):
                ring_copies[way, turns - 1, part].wait_recv()
            value = value + last_in[way]
        grad_ref[...] = value

    step_copies = []

    def adam(y):
        low = y * piece
        here = pl.multiple_of(rep * shard + low, piece)
        total = wg[pl.ds(here, piece), :]
        for peer in range(0 if mirror else reps - 1):
            wg_copies[peer, y].wait_recv()
            total = total + wg_in[peer, low : low + piece, :].astype(F32)
        sum_ref[low : low + piece, :] = total
        new_first = beta_first * first[low : low + piece, :] + (1.0 - beta_first) * total
        new_second = beta_second * second[low : low + piece, :] + (1.0 - beta_second) * total * total
        first_hat = new_first * (1.0 / (1.0 - beta_first**step_count))
        second_hat = new_second * (1.0 / (1.0 - beta_second**step_count))
        step_ref[pl.ds(here, piece), :] = (
            first_hat / (jnp.sqrt(second_hat) + adam_epsilon)
        ).astype(BF16)
        for peer in range(reps - 1):
            step_copies.append(
                remote(
                    step_ref.at[pl.ds(here, piece)], step_ref.at[pl.ds(here, piece)],
                    step_send, step_recv, peer * pieces + y, partners[peer],
                )
            )

    ring_step(0)
    if mirror:
        pick_turn(0, 1)
        pick_turn(1, 1)
    ring_step(1)
    if mirror:
        far_arrived(turns - 1, in_order[0:2])
        for turn in range(2, turns - 1):
            far_arrived(turn)
        far_arrived(turns - 1, in_order[2:4])
        for turn in range(2, turns):
            pick_turn(turn, 1)
        ring_step(2)
        far_arrived(turns)
        pick_turn(turns, 1)
        for y in range(pieces):
            far_block(y)
            adam(y)
        for s in range(3, turns):
            ring_step(s)
        ring_end()
    else:
        for k in range(max(pieces, turns - 1)):
            if k < pieces:
                adam(k)
            if k + 2 < turns:
                ring_step(k + 2)
            if k + 2 == turns:
                ring_end()

    for copies in (gathers, twins):
        for group in copies.values():
            for copy in group:
                copy.wait_send()
    for copies in (part_copies, ring_copies, wg_copies):
        for copy in copies.values():
            copy.wait_send()
    for copy in step_copies:
        copy.wait_send()
        copy.wait_recv()


def body(reps, labs, queries, shortlist, positive, label_weight, first_moment, second_moment):
    rows, depth = queries.shape
    names = shortlist.shape[1]
    local = label_weight.shape[0]
    shard = first_moment.shape[1]
    chips = labs // 2
    turns = chips // 2
    blocks = local // BLOCK
    piece = min(shard, BLOCK)
    pieces = shard // piece
    info = jnp.concatenate([shortlist.T, positive.T], axis=0).astype(BF16)
    vmem = pl.BlockSpec(memory_space=pltpu.VMEM)
    anywhere = pl.BlockSpec(memory_space=pl.ANY)
    dma = pltpu.SemaphoreType.DMA
    scratch = [
        pltpu.VMEM((labs * rows, depth), BF16),
        pltpu.VMEM((labs, 2 * names, rows), BF16),
        pltpu.VMEM((local, depth), F32),
        pltpu.VMEM((blocks, labs * CAP, depth), BF16),
        pltpu.VMEM((blocks, labs * CAP, BLOCK), F32),
        pltpu.VMEM((chips, blocks * 2 * CAP, 2 * rows), BF16),
        pltpu.VMEM((blocks, labs * CAP, depth), F32),
        pltpu.VMEM((2 * rows, 2 * rows), BF16),
        pltpu.VMEM((chips, rows, depth), F32),
        pltpu.VMEM((chips, rows, depth), F32),
        pltpu.VMEM((chips, rows, depth), F32),
        pltpu.VMEM((2 * turns, rows, depth), BF16),
        pltpu.VMEM((2 * turns, rows, depth), BF16),
        pltpu.VMEM((2, rows, depth), F32),
        pltpu.VMEM((2, rows, depth), F32),
        pltpu.VMEM((reps - 1, shard, depth), BF16),
        pltpu.VMEM((reps - 1, shard, depth), BF16),
        pltpu.VMEM((shard, depth), F32),
        pltpu.VMEM((shard, depth), F32),
    ]
    far_labs, far_blocks = (labs, shard // BLOCK) if mirrored(reps, shard) else (1, 1)
    scratch += [
        pltpu.VMEM((far_labs * rows, depth), BF16),
        pltpu.VMEM((far_labs, 2 * names, rows), BF16),
        pltpu.VMEM((far_blocks, far_labs * CAP, depth), BF16),
        pltpu.VMEM((far_blocks, far_labs * CAP, BLOCK), F32),
    ]
    scratch += [dma((8 * turns + 4,))] * 8
    scratch += [dma((chips,))] * 2 + [dma((4 * turns,))] * 2
    scratch += [dma(((reps - 1) * pieces,))] * 4 + [dma((2,))]
    scratch += [dma((4 * turns + 2,))] * 4
    grad, step, total = pl.pallas_call(
        functools.partial(kernel, reps, labs, rows, depth, names, local, shard),
        out_shape=(
            jax.ShapeDtypeStruct((rows, depth), F32),
            jax.ShapeDtypeStruct((local, depth), BF16),
            jax.ShapeDtypeStruct((shard, depth), F32),
        ),
        in_specs=[vmem, vmem, vmem, anywhere, anywhere],
        out_specs=(vmem, vmem, vmem),
        scratch_shapes=scratch,
        compiler_params=pltpu.CompilerParams(
            collective_id=0, has_side_effects=True, vmem_limit_bytes=56 * 1024 * 1024
        ),
    )(queries, info, label_weight, first_moment[0], second_moment[0])
    total = total[None]
    new_first = beta_first * first_moment + (1.0 - beta_first) * total
    new_second = beta_second * second_moment + (1.0 - beta_second) * total * total
    new_weight = label_weight.astype(F32) - learn_rate * step.astype(F32)
    return (grad, new_weight, new_first, new_second)


def solution(mesh):
    in_specs = (
        P(("rep", "lab"), None),
        P(("rep", "lab"), None),
        P(("rep", "lab"), None),
        P("lab", None),
        P("rep", "lab", None),
        P("rep", "lab", None),
    )
    out_specs = (
        P(("rep", "lab"), None),
        P("lab", None),
        P("rep", "lab", None),
        P("rep", "lab", None),
    )
    run = functools.partial(body, mesh.shape["rep"], mesh.shape["lab"])
    return jax.shard_map(run, mesh=mesh, in_specs=in_specs, out_specs=out_specs, check_vma=False)
```

```python
import functools

import jax
import jax.numpy as jnp
from jax import lax
from jax.experimental import pallas as pl
from jax.experimental.pallas import tpu as pltpu
from jax.sharding import PartitionSpec as P

BLOCK = 128
CAP = 8
F32 = jnp.float32
BF16 = jnp.bfloat16
MESH = pl.DeviceIdType.MESH

beta_first = 0.9
beta_second = 0.999
learn_rate = 0.01
adam_epsilon = 1e-08
step_count = 100.0


def chip_at(place, chips):
    place = lax.rem(place + 2 * chips, chips)
    back = lax.div(place, chips // 2)
    return 2 * place + back * (2 * (chips - 1 - place) + 1 - 2 * place)


def mirrored(reps, shard):
    return reps == 2 and shard % BLOCK == 0


def kernel(
    reps, labs, rows, depth, names, local, shard,
    q_ref, info_ref, w_ref, first_ref, second_ref,
    grad_ref, step_ref, sum_ref,
    qbuf, ibuf, wg, gbuf, mbuf, pbuf, qslot, earlier, own_part, pair_out, pair_in,
    ring_out, ring_in, last_out, last_in, wg_out, wg_in, first, second,
    far_q, far_i, far_g, far_m,
    gather_send, gather_recv, note_send, note_recv,
    twin_send, twin_recv, twin_note_send, twin_note_recv,
    part_send, part_recv, ring_send, ring_recv,
    wg_send, wg_recv, step_send, step_recv, load_sem,
    cross_send, cross_recv, cross_note_send, cross_note_recv,
):
    chips = labs // 2
    turns = chips // 2
    half = rows // 2
    blocks = local // BLOCK
    piece = min(shard, BLOCK)
    pieces = shard // piece
    rep = lax.axis_index("rep")
    lab = lax.axis_index("lab")
    core = lax.rem(lab, 2)
    chip = lax.div(lab, 2)
    odd = lax.rem(chip, 2)
    rank = lax.div(chip, 2)
    place = rank + odd * (chips - 1 - 2 * rank)
    ahead = (rep, chip_at(place + 1, chips) * 2 + core)
    behind = (rep, chip_at(place - 1, chips) * 2 + core)
    twin = (rep, chip * 2 + 1 - core)
    partners = [(lax.rem(rep + j, reps), lab) for j in range(1, reps)]

    load_first = pltpu.make_async_copy(first_ref, first, load_sem.at[0])
    load_second = pltpu.make_async_copy(second_ref, second, load_sem.at[1])
    load_first.start()
    load_second.start()

    barrier = pltpu.get_barrier_semaphore()
    everyone = [ahead, behind, twin] + partners
    for other in everyone:
        pl.semaphore_signal(barrier, inc=1, device_id=other, device_id_type=MESH)
    qbuf[0:rows, :] = q_ref[...]
    ibuf[0] = info_ref[...]
    pl.semaphore_wait(barrier, len(everyone))

    def remote(src, dst, send, recv, index, device):
        copy = pltpu.make_async_remote_copy(
            src_ref=src, dst_ref=dst, send_sem=send.at[index], recv_sem=recv.at[index],
            device_id=device, device_id_type=MESH,
        )
        copy.start()
        return copy

    def chunk(way, turn):
        if turn == 0:
            return 0
        if turn == turns:
            return 2 + 4 * (turns - 1)
        return 2 + 4 * (turn - 1) + 2 * way

    def sem(way, turn):
        return 2 * turn - 1 + way if turn else 0

    mirror = mirrored(reps, shard)
    own_first = rep * (shard // BLOCK)
    crossing = (0, 1, turns - 1)
    both = ((qbuf, ibuf, 0), (far_q, far_i, 4 * turns + 2))
    gathers, twins = {}, {}
    slots = 2 * CAP

    def halves(way, turn):
        return (way,) if turn == turns else (0, 1)

    def send_on(way, turn, part, far=0):
        qb, ib, base = both[far]
        src, dst = chunk(way, turn - 1), chunk(way, turn)
        k = base + 2 * sem(way, turn) + part
        device = ahead if way == 0 else behind
        low = part * half
        got = [
            remote(
                qb.at[pl.ds(src * rows + low, half)], qb.at[pl.ds(dst * rows + low, half)],
                gather_send, gather_recv, k, device,
            )
        ]
        if part == 0:
            got.append(remote(ib.at[src], ib.at[dst], note_send, note_recv, k, device))
        gathers[way, turn, part, far] = got

    def send_across(way, turn, part):
        c = chunk(way, turn)
        k = 2 * sem(way, turn) + part
        here = pl.ds(c * rows + part * half, half)
        got = [remote(qbuf.at[here], far_q.at[here], cross_send, cross_recv, k, partners[0])]
        if part == 0:
            got.append(
                remote(ibuf.at[c], far_i.at[c], cross_note_send, cross_note_recv, k, partners[0])
            )
        gathers[way, turn, part, 1] = got

    def send_twin(way, turn, part, far=0):
        qb, ib, base = both[far]
        c = chunk(way, turn)
        k = base + 2 * sem(way, turn) + part
        low = part * half
        got = [
            remote(
                qb.at[pl.ds(c * rows + low, half)], qb.at[pl.ds((c + 1) * rows + low, half)],
                twin_send, twin_recv, k, twin,
            )
        ]
        if part == 0:
            got.append(remote(ib.at[c], ib.at[c + 1], twin_note_send, twin_note_recv, k, twin))
        twins[way, turn, part, far] = got

    def pair_of(way, turn):
        return chunk(way, turn) // 2

    def pick(i, far=0):
        qb, ib, _ = both[far]
        count = shard // BLOCK if far else blocks
        block0 = lab * blocks + (own_first if far else 0)
        gb, mb = (far_g, far_m) if far else (gbuf, mbuf)
        width = 2 * rows
        pair = (2 * i, 2 * i + 1)
        listed = jnp.concatenate([ib[c, 0:names, :] for c in pair], axis=1).astype(F32)
        wanted = jnp.concatenate([ib[c, names : 2 * names, :] for c in pair], axis=1).astype(F32)
        hits, marks = [], []
        for b in range(count):
            same = listed == (block0 + b).astype(F32)
            hits.append(jnp.sum(jnp.where(same, 1.0, 0.0), axis=0, keepdims=True))
            marks.append(jnp.sum(jnp.where(same, wanted + 1.0, 0.0), axis=0, keepdims=True))
        hit = jnp.concatenate(hits, axis=0)
        later = lax.broadcasted_iota(jnp.int32, (count, width), 1) >= rows
        order = jnp.dot(hit.astype(BF16), earlier[...], preferred_element_type=F32)
        order = order + jnp.where(later, float(CAP), 0.0)
        order = jnp.where(hit > 0.0, order, -1.0)
        number = lax.broadcasted_iota(jnp.int32, (slots, width), 0).astype(F32)
        chosen = []
        for b in range(count):
            mine = number == order[b : b + 1, :]
            mark = jnp.sum(jnp.where(mine, marks[b], 0.0), axis=1, keepdims=True)
            mb[b, i * slots : (i + 1) * slots, :] = jnp.broadcast_to(mark, (slots, BLOCK))
            chosen.append(jnp.where(mine, 1.0, 0.0))
        select = jnp.concatenate(chosen, axis=0).astype(BF16)
        if not far:
            pbuf[i] = select
        picked = jnp.dot(
            select, qb[2 * i * rows : 2 * (i + 1) * rows, :], preferred_element_type=F32
        ).astype(BF16)
        for b in range(count):
            gb[b, i * slots : (i + 1) * slots, :] = picked[b * slots : (b + 1) * slots, :]

    def slopes_of(rows_in, weights, mark):
        logits = lax.dot_general(
            rows_in, weights, (((1,), (1,)), ((), ())), preferred_element_type=F32
        )
        offsets = lax.broadcasted_iota(jnp.int32, mark.shape, 1).astype(F32) + 1.0
        target = (offsets == mark).astype(F32)
        return jnp.where(mark > 0.0, jax.nn.sigmoid(logits) - target, 0.0).astype(BF16)

    def weight_part(slopes, rows_in):
        return lax.dot_general(
            slopes, rows_in, (((0,), (0,)), ((), ())), preferred_element_type=F32
        )

    def one_block(b, with_weights=True):
        rows_in = gbuf[b]
        here = pl.multiple_of(b * BLOCK, BLOCK)
        weights = w_ref[pl.ds(here, BLOCK), :]
        slopes = slopes_of(rows_in, weights, mbuf[b])
        if with_weights:
            wg[pl.ds(here, BLOCK), :] = weight_part(slopes, rows_in)
        qslot[b] = jnp.dot(slopes, weights, preferred_element_type=F32)

    def far_block(j):
        rows_in = far_g[j]
        here = pl.multiple_of((own_first + j) * BLOCK, BLOCK)
        slopes = slopes_of(rows_in, w_ref[pl.ds(here, BLOCK), :], far_m[j])
        wg[pl.ds(here, BLOCK), :] = wg[pl.ds(here, BLOCK), :] + weight_part(slopes, rows_in)

    part_copies = {}

    def row_parts(i):
        slot_grad = jnp.concatenate(
            [qslot[b, i * slots : (i + 1) * slots, :] for b in range(blocks)], axis=0
        )
        high = slot_grad.astype(BF16)
        low = (slot_grad - high.astype(F32)).astype(BF16)
        dims = (((0,), (0,)), ((), ()))
        part = lax.dot_general(pbuf[i], high, dims, preferred_element_type=F32)
        part = part + lax.dot_general(pbuf[i], low, dims, preferred_element_type=F32)
        own_part[i] = part[0:rows]
        pair_out[i] = part[rows : 2 * rows]
        part_copies[i] = remote(pair_out.at[i], pair_in.at[i], part_send, part_recv, i, twin)

    def pick_turn(turn, far=0):
        for way in (0, 1):
            for part in halves(way, turn):
                if (way, turn, part, far) in twins:
                    for copy in twins[way, turn, part, far]:
                        copy.wait_recv()
        pick(pair_of(0, turn), far)
        if 0 < turn < turns:
            pick(pair_of(1, turn), far)

    in_order = ((0, 0), (1, 1), (0, 1), (1, 0))

    def cross_turn(turn):
        for way, part in in_order:
            if turn or not way:
                send_across(way, turn, part)

    def far_arrived(turn, cases=in_order):
        for way, part in cases:
            if (way, turn, part, 1) not in gathers:
                continue
            for copy in gathers[way, turn, part, 1]:
                copy.wait_recv()
            following = turn + 1
            if following <= turns and following not in crossing:
                for on in (0, 1) if turn == 0 else (way,):
                    if part in halves(on, following):
                        send_on(on, following, part, 1)
            send_twin(way, turn, part, 1)

    for part in (0, 1):
        send_on(0, 1, part)
        send_on(1, 1, part)
    if mirror:
        cross_turn(0)
    for part in (0, 1):
        send_twin(0, 0, part)
    below = lax.broadcasted_iota(jnp.int32, (2 * rows, 2 * rows), 0)
    right = lax.broadcasted_iota(jnp.int32, (2 * rows, 2 * rows), 1)
    one_shard = lax.div(below, rows) == lax.div(right, rows)
    earlier[...] = jnp.where((below < right) & one_shard, 1.0, 0.0).astype(BF16)
    for turn in range(1, turns + 1):
        for part in (0, 1):
            for way in (0, 1):
                if (way, turn, part, 0) not in gathers:
                    continue
                for copy in gathers[way, turn, part, 0]:
                    copy.wait_recv()
                if turn < turns and part in halves(way, turn + 1):
                    send_on(way, turn + 1, part)
                send_twin(way, turn, part)
        if mirror and turn in crossing:
            cross_turn(turn)
        pick_turn(turn - 1)
        if mirror and turn == turns - 1:
            for far_turn in (0, 1):
                far_arrived(far_turn)
    if mirror:
        far_arrived(turns - 1, in_order[0:2])
    pick_turn(turns)

    wg_copies = {}

    def wg_send_on(peer, y):
        low = y * piece
        start = pl.multiple_of(lax.rem(rep + 1 + peer, reps) * shard + low, piece)
        wg_out[peer, low : low + piece, :] = wg[pl.ds(start, piece), :].astype(BF16)
        wg_copies[peer, y] = remote(
            wg_out.at[peer, pl.ds(low, piece)], wg_in.at[peer, pl.ds(low, piece)],
            wg_send, wg_recv, peer * pieces + y, partners[peer],
        )

    if mirror:
        per_shard = shard // BLOCK
        for j in range(blocks):
            peer = j // per_shard
            one_block(lax.rem(rep + 1 + peer, reps) * per_shard + j % per_shard, peer > 0)
    elif shard >= BLOCK:
        per_shard = shard // BLOCK
        for j in range(blocks):
            peer = j // per_shard
            one_block(lax.rem(rep + 1 + peer, reps) * per_shard + j % per_shard)
            if peer < reps - 1:
                wg_send_on(peer, j % per_shard)
    else:
        for b in range(blocks):
            one_block(b)
        for peer in range(reps - 1):
            wg_send_on(peer, 0)
    load_first.wait()
    load_second.wait()

    ring_copies = {}

    def ring_step(s):
        for way in (0, 1):
            i = pair_of(1 - way, turns - s)
            if s > 0 or way == 0:
                part_copies[i].wait_recv()
            k = way * turns + s
            device = ahead if way == 0 else behind
            if s == 0:
                low = half * way
                value = own_part[i, low : low + half, :] + pair_in[i, low : low + half, :]
                ring_out[k, 0:half, :] = value.astype(BF16)
                ring_copies[way, s] = remote(
                    ring_out.at[k, pl.ds(0, half)], ring_in.at[k, pl.ds(0, half)],
                    ring_send, ring_recv, k, device,
                )
                continue
            ring_copies[way, s - 1].wait_recv()
            value = own_part[i] + pair_in[i]
            if s == 1:
                low = half * way
                mixed = [value[0:half], value[half:rows]]
                mixed[way] = mixed[way] + ring_in[k - 1, 0:half, :].astype(F32)
                value = jnp.concatenate(mixed, axis=0)
            else:
                value = value + ring_in[k - 1].astype(F32)
            if s == turns - 1:
                last_out[way] = value
                ring_copies[way, s] = remote(
                    last_out.at[way], last_in.at[way], ring_send, ring_recv, k, device
                )
            else:
                ring_out[k] = value.astype(BF16)
                ring_copies[way, s] = remote(
                    ring_out.at[k], ring_in.at[k], ring_send, ring_recv, k, device
                )

    def ring_end():
        part_copies[0].wait_recv()
        value = own_part[0] + pair_in[0]
        for way in (0, 1):
            ring_copies[way, turns - 1].wait_recv()
            value = value + last_in[way]
        grad_ref[...] = value

    step_copies = []

    def adam(y):
        low = y * piece
        here = pl.multiple_of(rep * shard + low, piece)
        total = wg[pl.ds(here, piece), :]
        for peer in range(0 if mirror else reps - 1):
            wg_copies[peer, y].wait_recv()
            total = total + wg_in[peer, low : low + piece, :].astype(F32)
        sum_ref[low : low + piece, :] = total
        new_first = beta_first * first[low : low + piece, :] + (1.0 - beta_first) * total
        new_second = beta_second * second[low : low + piece, :] + (1.0 - beta_second) * total * total
        first_hat = new_first * (1.0 / (1.0 - beta_first**step_count))
        second_hat = new_second * (1.0 / (1.0 - beta_second**step_count))
        step_ref[pl.ds(here, piece), :] = (
            first_hat / (jnp.sqrt(second_hat) + adam_epsilon)
        ).astype(BF16)
        for peer in range(reps - 1):
            step_copies.append(
                remote(
                    step_ref.at[pl.ds(here, piece)], step_ref.at[pl.ds(here, piece)],
                    step_send, step_recv, peer * pieces + y, partners[peer],
                )
            )

    def parts_back(turn):
        for way in (0,) if turn in (0, turns) else (0, 1):
            row_parts(pair_of(way, turn))

    parts_back(turns)
    parts_back(turns - 1)
    ring_step(0)
    for turn in range(turns - 2, -1, -1):
        parts_back(turn)
    if mirror:
        pick_turn(0, 1)
        pick_turn(1, 1)
        ring_step(1)
        far_arrived(turns - 1, in_order[2:4])
        for turn in range(2, turns - 1):
            far_arrived(turn)
        for turn in range(2, turns):
            pick_turn(turn, 1)
        ring_step(2)
        far_arrived(turns)
        pick_turn(turns, 1)
        for y in range(pieces):
            far_block(y)
            adam(y)
        for s in range(3, turns):
            ring_step(s)
        ring_end()
    else:
        ring_step(1)
        for k in range(max(pieces, turns - 1)):
            if k < pieces:
                adam(k)
            if k + 2 < turns:
                ring_step(k + 2)
            if k + 2 == turns:
                ring_end()

    for copies in (gathers, twins):
        for group in copies.values():
            for copy in group:
                copy.wait_send()
    for copies in (part_copies, ring_copies, wg_copies):
        for copy in copies.values():
            copy.wait_send()
    for copy in step_copies:
        copy.wait_send()
        copy.wait_recv()


def body(reps, labs, queries, shortlist, positive, label_weight, first_moment, second_moment):
    rows, depth = queries.shape
    names = shortlist.shape[1]
    local = label_weight.shape[0]
    shard = first_moment.shape[1]
    chips = labs // 2
    turns = chips // 2
    blocks = local // BLOCK
    piece = min(shard, BLOCK)
    pieces = shard // piece
    info = jnp.concatenate([shortlist.T, positive.T], axis=0).astype(BF16)
    vmem = pl.BlockSpec(memory_space=pltpu.VMEM)
    anywhere = pl.BlockSpec(memory_space=pl.ANY)
    dma = pltpu.SemaphoreType.DMA
    scratch = [
        pltpu.VMEM((labs * rows, depth), BF16),
        pltpu.VMEM((labs, 2 * names, rows), BF16),
        pltpu.VMEM((local, depth), F32),
        pltpu.VMEM((blocks, labs * CAP, depth), BF16),
        pltpu.VMEM((blocks, labs * CAP, BLOCK), F32),
        pltpu.VMEM((chips, blocks * 2 * CAP, 2 * rows), BF16),
        pltpu.VMEM((blocks, labs * CAP, depth), F32),
        pltpu.VMEM((2 * rows, 2 * rows), BF16),
        pltpu.VMEM((chips, rows, depth), F32),
        pltpu.VMEM((chips, rows, depth), F32),
        pltpu.VMEM((chips, rows, depth), F32),
        pltpu.VMEM((2 * turns, rows, depth), BF16),
        pltpu.VMEM((2 * turns, rows, depth), BF16),
        pltpu.VMEM((2, rows, depth), F32),
        pltpu.VMEM((2, rows, depth), F32),
        pltpu.VMEM((reps - 1, shard, depth), BF16),
        pltpu.VMEM((reps - 1, shard, depth), BF16),
        pltpu.VMEM((shard, depth), F32),
        pltpu.VMEM((shard, depth), F32),
    ]
    far_labs, far_blocks = (labs, shard // BLOCK) if mirrored(reps, shard) else (1, 1)
    scratch += [
        pltpu.VMEM((far_labs * rows, depth), BF16),
        pltpu.VMEM((far_labs, 2 * names, rows), BF16),
        pltpu.VMEM((far_blocks, far_labs * CAP, depth), BF16),
        pltpu.VMEM((far_blocks, far_labs * CAP, BLOCK), F32),
    ]
    scratch += [dma((8 * turns + 4,))] * 8
    scratch += [dma((chips,))] * 2 + [dma((2 * turns,))] * 2
    scratch += [dma(((reps - 1) * pieces,))] * 4 + [dma((2,))]
    scratch += [dma((4 * turns + 2,))] * 4
    grad, step, total = pl.pallas_call(
        functools.partial(kernel, reps, labs, rows, depth, names, local, shard),
        out_shape=(
            jax.ShapeDtypeStruct((rows, depth), F32),
            jax.ShapeDtypeStruct((local, depth), BF16),
            jax.ShapeDtypeStruct((shard, depth), F32),
        ),
        in_specs=[vmem, vmem, vmem, anywhere, anywhere],
        out_specs=(vmem, vmem, vmem),
        scratch_shapes=scratch,
        compiler_params=pltpu.CompilerParams(
            collective_id=0, has_side_effects=True, vmem_limit_bytes=56 * 1024 * 1024
        ),
    )(queries, info, label_weight, first_moment[0], second_moment[0])
    total = total[None]
    new_first = beta_first * first_moment + (1.0 - beta_first) * total
    new_second = beta_second * second_moment + (1.0 - beta_second) * total * total
    new_weight = label_weight.astype(F32) - learn_rate * step.astype(F32)
    return (grad, new_weight, new_first, new_second)


def solution(mesh):
    in_specs = (
        P(("rep", "lab"), None),
        P(("rep", "lab"), None),
        P(("rep", "lab"), None),
        P("lab", None),
        P("rep", "lab", None),
        P("rep", "lab", None),
    )
    out_specs = (
        P(("rep", "lab"), None),
        P("lab", None),
        P("rep", "lab", None),
        P("rep", "lab", None),
    )
    run = functools.partial(body, mesh.shape["rep"], mesh.shape["lab"])
    return jax.shard_map(run, mesh=mesh, in_specs=in_specs, out_specs=out_specs, check_vma=False)
```
